256 devices in a mesh: slab: 64 (over y_hi, z, x), cross: 4 (over y_lo, core).
Axes of the slice: x: 4, y: 4 (y_hi: 2, y_lo: 2; y = y_hi * 2 + y_lo), z: 8, core: 2. Of those that a mesh axis runs over, the one named last changes fastest.
Arguments:
- features: bfloat16 [128, 8, 30, 128], P('slab', 'cross'), may hold values from -6 to 6
- position: float32 [128, 8, 2, 128], P('slab', 'cross'), may hold values from -6 to 6
- velocity: float32 [128, 8, 2, 128], P('slab', 'cross'), may hold values from -6 to 6
- occupancy: int32 [128, 8], P('slab', 'cross'), may hold values from 32 to 128
- neighbor_codes: int32 [128, 8, 16, 128], P('slab', 'cross'), may hold values from 0 to 1151
- edge_mask: int32 [128, 8, 16, 128], P('slab', 'cross'), may hold values 0 or 1
- enc_first: bfloat16 [30, 128], replicated, may hold values from -1 to 1
- enc_second: bfloat16 [128, 128], replicated, may hold values from -0.5 to 0.5
- edge_recv: bfloat16 [3, 128, 512], replicated, may hold values from -0.5 to 0.5
- edge_send: bfloat16 [3, 128, 512], replicated, may hold values from -0.5 to 0.5
- edge_geo: float32 [3, 3, 512], replicated, may hold values from -3.5 to 3.5
- edge_out: bfloat16 [3, 512, 128], replicated, may hold values from -0.25 to 0.25
- node_first: bfloat16 [3, 256, 128], replicated, may hold values from -0.375 to 0.375
- node_second: bfloat16 [3, 128, 128], replicated, may hold values from -0.5 to 0.5
- dec_first: bfloat16 [128, 128], replicated, may hold values from -0.5 to 0.5
- dec_second: bfloat16 [128, 2], replicated, may hold values from -0.5 to 0.5
Outputs:
- new_velocity: float32 [128, 8, 2, 128], P('slab', 'cross')
- new_position: float32 [128, 8, 2, 128], P('slab', 'cross')
The draws below stay inside these ranges and needn't reach their ends.
Inputs may be any that keep to these rules, and one draw needn't show every extreme that they name: `neighbor_codes`: entries name slots of the 3 x 3 bins around a slot's own bin, encoded as in the reference program; some name dead or outside slots.
All inputs are finite; a program needn't handle non-finite values. No bound on the sum of `edge_mask` on one device may be relied on, other than what follows from the above.
Results may differ from the reference program's by a relative error of at most 0.015.
Values may be sent and summed in bfloat16 or wider, within the bound.
No kernel may reach another device: no remote copies, remote signals or barrier semaphores. Data moves between devices by JAX's collectives and lax.ppermute only.
A program may use at most 64 MiB of HBM per device.

```python
import jax
import jax.numpy as jnp
from jax import lax

LAT = 128
EH = 512
INF = 30
SLOTS = 128
KNB = 16
STEPS = 3
NBX = 128
NBY = 8


def touch_ends(values, rng, low, high):
    longest = values.shape.index(max(values.shape))
    spots = []
    for shift in (0, 1):
        where = [jax.random.randint(jax.random.fold_in(rng, axis), (), 0, length) for axis, length in enumerate(values.shape)]
        where[longest] = (where[longest] + shift) % values.shape[longest]
        spots.append(tuple(where))
    return values.at[spots[0]].set(low).at[spots[1]].set(high)


def levels(own_key, shape, shards, low, top_value):
    def one(dim, parts):
        draws = jax.random.uniform(jax.random.fold_in(jax.random.fold_in(own_key, 6), dim), (parts,), jnp.float32, low / len(shards), top_value / len(shards))
        return jnp.repeat(jnp.exp(draws), shape[dim] // parts).reshape((-1,) + (1,) * (len(shape) - dim - 1))

    factor_of = one(*shards[0])
    for cut in shards[1:]:
        factor_of = factor_of * one(*cut)
    return factor_of


def scatter_about(key, extent, scale, bound, cuts=(), held_as=jnp.bfloat16):
    values = jax.random.normal(key, extent, jnp.float32) * scale
    if len(cuts) > 0:
        values = levels(key, extent, cuts, -0.22, 0.18) * values
    return jnp.clip(values, min=-bound, max=bound).astype(held_as)


def setup_inputs(seed: int = 0) -> dict:
    streams_of = jax.random.split(jax.random.key(seed), 17)
    return {
        "features": scatter_about(streams_of[0], (NBX, NBY, INF, SLOTS), 1.0, 6.0, ((0, 64), (1, 4))),
        "position": scatter_about(streams_of[1], (NBX, NBY, 2, SLOTS), 1.0, 6.0, ((0, 64), (1, 4)), jnp.float32),
        "velocity": scatter_about(streams_of[2], (NBX, NBY, 2, SLOTS), 1.0, 6.0, ((0, 64), (1, 4)), jnp.float32),
        "occupancy": touch_ends(jax.random.randint(streams_of[3], (NBX, NBY), SLOTS // 4, SLOTS + 1), jax.random.fold_in(streams_of[3], 1), SLOTS // 4, SLOTS).astype(jnp.int32),
        "neighbor_codes": touch_ends(jax.random.randint(streams_of[4], (NBX, NBY, KNB, SLOTS), 0, 9 * SLOTS), jax.random.fold_in(streams_of[4], 1), 0, (9 * SLOTS) - 1).astype(jnp.int32),
        "edge_mask": touch_ends((jax.random.randint(streams_of[5], (NBX, NBY, KNB, SLOTS), 0, 4) < 3).astype(jnp.int32), jax.random.fold_in(streams_of[5], 1), 0, 1),
        "enc_first": scatter_about(streams_of[6], (INF, LAT), INF ** -0.5, 1.0),
        "enc_second": scatter_about(streams_of[7], (LAT, LAT), LAT ** -0.5, 0.5),
        "edge_recv": scatter_about(streams_of[8], (STEPS, LAT, EH), LAT ** -0.5, 0.5),
        "edge_send": scatter_about(streams_of[9], (STEPS, LAT, EH), LAT ** -0.5, 0.5),
        "edge_geo": scatter_about(streams_of[10], (STEPS, 3, EH), 3 ** -0.5, 3.5, (), jnp.float32),
        "edge_out": scatter_about(streams_of[11], (STEPS, EH, LAT), EH ** -0.5, 0.25),
        "node_first": scatter_about(streams_of[12], (STEPS, 2 * LAT, LAT), (2 * LAT) ** -0.5, 0.375),
        "node_second": scatter_about(streams_of[13], (STEPS, LAT, LAT), LAT ** -0.5, 0.5),
        "dec_first": scatter_about(streams_of[14], (LAT, LAT), LAT ** -0.5, 0.5),
        "dec_second": scatter_about(streams_of[15], (LAT, 2), LAT ** -0.5, 0.5),
    }


time_step = 0.5

def layer_norm(values):
    center = values - lax.optimization_barrier(jnp.mean(values, axis=-1, keepdims=True))
    spread = lax.optimization_barrier(jnp.mean(center * center, axis=-1, keepdims=True))
    return center * lax.rsqrt(spread + 1e-05)

def neighbor_rows(codes, slot_count, rows_y):
    bin_code = codes // slot_count
    slot_code = codes % slot_count
    shift_x = bin_code // 3 - 1
    shift_y = bin_code % 3 - 1
    index_x = lax.broadcasted_iota(jnp.int32, codes.shape, 0)
    index_y = lax.broadcasted_iota(jnp.int32, codes.shape, 1)
    flat = ((index_x + 1 + shift_x) * (rows_y + 2) + index_y + 1 + shift_y) * slot_count + slot_code
    return flat.reshape(-1).astype(jnp.int32)

def message_step(latent, padded_send, geo_rows, own_geo, codes, edge_mask, recv_weight, geo_weight, out_weight, first_weight, second_weight):
    size_x, size_y, slot_count, width = latent.shape
    flat = latent.reshape(-1, width)
    recv_proj = jnp.dot(flat, recv_weight, preferred_element_type=jnp.float32).astype(jnp.bfloat16)
    send_rows = padded_send.reshape(-1, padded_send.shape[-1])
    live_own = own_geo[:, 2]
    total = jnp.zeros((flat.shape[0], width), jnp.float32)
    for column in range(codes.shape[2]):
        rows = neighbor_rows(codes[:, :, column, :], slot_count, size_y)
        sender = jnp.take(send_rows, rows, axis=0)
        other = jnp.take(geo_rows, rows, axis=0)
        delta_x = other[:, 0] - own_geo[:, 0]
        delta_y = other[:, 1] - own_geo[:, 1]
        distance = delta_x * delta_x + delta_y * delta_y
        geo_term = delta_x[:, None] * geo_weight[0] + delta_y[:, None] * geo_weight[1] + distance[:, None] * geo_weight[2]
        hidden = jax.nn.relu(recv_proj.astype(jnp.float32) + sender.astype(jnp.float32) + geo_term).astype(jnp.bfloat16)
        message = jnp.dot(hidden, out_weight, preferred_element_type=jnp.float32)
        valid = edge_mask[:, :, column, :].reshape(-1).astype(jnp.float32) * live_own * other[:, 2]
        total = total + valid[:, None] * message
    summed = total.astype(jnp.bfloat16)
    joined = jnp.dot(flat, first_weight[:width], preferred_element_type=jnp.float32) + jnp.dot(summed, first_weight[width:], preferred_element_type=jnp.float32)
    joined = jax.nn.relu(joined).astype(jnp.bfloat16)
    update = jnp.dot(joined, second_weight, preferred_element_type=jnp.float32)
    result = (flat.astype(jnp.float32) + layer_norm(update)).astype(jnp.bfloat16)
    return result.reshape(latent.shape)

def reference(features, position, velocity, occupancy, neighbor_codes, edge_mask, enc_first, enc_second, edge_recv, edge_send, edge_geo, edge_out, node_first, node_second, dec_first, dec_second):
    size_x, size_y, count_two, slot_count = position.shape
    slot_index = lax.broadcasted_iota(jnp.int32, (size_x, size_y, 1, slot_count), 3)
    live = (slot_index < occupancy[:, :, None, None]).astype(jnp.float32)
    geometry = jnp.concatenate([position, live], axis=2)
    padded_geo = jnp.pad(geometry, ((1, 1), (1, 1), (0, 0), (0, 0)))
    geo_rows = jnp.transpose(padded_geo, (0, 1, 3, 2)).reshape(-1, 3)
    own_geo = jnp.transpose(geometry, (0, 1, 3, 2)).reshape(-1, 3)
    enc_hidden = jax.nn.relu(jnp.einsum('xyfs,fh->xysh', features.astype(jnp.float32), enc_first.astype(jnp.float32))).astype(jnp.bfloat16)
    width = enc_second.shape[0]
    latent = layer_norm(jnp.dot(enc_hidden.reshape(-1, width), enc_second, preferred_element_type=jnp.float32)).astype(jnp.bfloat16)
    latent = latent.reshape(size_x, size_y, slot_count, width)
    for layer_index in range(STEPS):
        send_proj = jnp.dot(latent.reshape(-1, width), edge_send[layer_index], preferred_element_type=jnp.float32).astype(jnp.bfloat16)
        send_proj = send_proj.reshape(size_x, size_y, slot_count, -1)
        padded_send = jnp.pad(send_proj, ((1, 1), (1, 1), (0, 0), (0, 0)))
        latent = message_step(latent, padded_send, geo_rows, own_geo, neighbor_codes, edge_mask, edge_recv[layer_index], edge_geo[layer_index], edge_out[layer_index], node_first[layer_index], node_second[layer_index])
    dec_hidden = jax.nn.relu(jnp.dot(latent.reshape(-1, width), dec_first, preferred_element_type=jnp.float32)).astype(jnp.bfloat16)
    accel = jnp.dot(dec_hidden, dec_second, preferred_element_type=jnp.float32)
    accel = jnp.transpose(accel.reshape(size_x, size_y, slot_count, 2), (0, 1, 3, 2)) * live
    new_velocity = velocity + time_step * accel
    new_position = position + time_step * new_velocity
    return (new_velocity, new_position)
```

```python
import functools

import jax
import jax.numpy as jnp
from jax import lax
from jax.experimental import pallas as pl
from jax.experimental.pallas import tpu as pltpu
from jax.sharding import PartitionSpec as P

time_step = 0.5
LAT = 128
EH = 512
KNB = 16
SLOTS = 128
PACK = 48
GEO = 16
BLOCKED = -(2.0**40)
bf16 = jnp.bfloat16
f32 = jnp.float32


def tdot(left, right):
    return lax.dot_general(left, right, (((0,), (0,)), ((), ())), preferred_element_type=f32)


def split(values):
    high = values.astype(bf16)
    low = (values - high.astype(f32)).astype(bf16)
    return high, low


def split3(values):
    high = values.astype(bf16)
    rest = values - high.astype(f32)
    mid = rest.astype(bf16)
    low = (rest - mid.astype(f32)).astype(bf16)
    return high, mid, low


def norm_rows(values):
    center = values - jnp.mean(values, axis=0, keepdims=True)
    spread = jnp.mean(center * center, axis=0, keepdims=True)
    return center * lax.rsqrt(spread + 1e-05)


def place(own, low, high, left, right, win, depth):
    for i in range(4):
        win[i, 0] = left[i, 0]
        win[i, 3] = right[i, 0]
        for j in range(2):
            if i == 0:
                win[i, j + 1] = low[0, j]
            elif i == 3:
                win[i, j + 1] = high[0, j]
            else:
                win[i, j + 1] = own[i - 1, j]


def one_hot(codes, pair):
    row = jnp.concatenate([codes[2 * pair : 2 * pair + 1], codes[2 * pair + 1 : 2 * pair + 2]], axis=1)
    window = row >> 7
    slot = row & (SLOTS - 1)
    iota = lax.broadcasted_iota(jnp.int32, (SLOTS, 2 * SLOTS), 0).astype(jnp.int16)
    parts = []
    for w in range(9):
        wanted = jnp.where(window == w, slot, -1).astype(jnp.int16)
        hit = iota == jnp.broadcast_to(wanted, (SLOTS, 2 * SLOTS))
        parts.append(jnp.where(hit, jnp.ones((), bf16), jnp.zeros((), bf16)))
    return jnp.concatenate(parts, axis=0)


def step_kernel(first, last, *refs):
    refs = list(refs)
    own, low, high, left, right = [refs.pop(0) for _ in range(5)]
    codes_ref = refs.pop(0)
    if first:
        mask_ref, position = refs.pop(0), refs.pop(0)
        enc_first, enc_second = refs.pop(0), refs.pop(0)
    else:
        geo_in = refs.pop(0)
    recv_w, send_w, geo_w, out_w, first_w, second_w = [refs.pop(0) for _ in range(6)]
    if last:
        occupancy, position, velocity, dec_first, dec_second = [refs.pop(0) for _ in range(5)]
        out_velocity, out_position = refs.pop(0), refs.pop(0)
    else:
        out_latent = refs.pop(0)
    if first:
        geo_out = refs.pop(0)
        pack = refs.pop(0)
    win, full_w, recv_all, sums = refs
    if first:
        place(own, low, high, left, right, pack, PACK)
        weight = jnp.concatenate([enc_first[...], jnp.zeros((PACK - 30, LAT), bf16)], axis=0)
        for i in range(4):
            raw = jnp.concatenate([pack[i, j] for j in range(4)], axis=1)
            hidden = jnp.maximum(tdot(weight, raw), 0.0).astype(bf16)
            latent = norm_rows(tdot(enc_second[...], hidden)).astype(bf16)
            for j in range(4):
                win[i, j] = latent[:, j * SLOTS : (j + 1) * SLOTS]
    else:
        place(own, low, high, left, right, win, LAT)
    own_all = jnp.concatenate([win[1 + b // 2, 1 + b % 2] for b in range(4)], axis=1)
    recv_all[...] = -tdot(recv_w[...], own_all)
    geo_high, geo_low = split(geo_w[...])
    rows = []
    for c in range(3):
        rows += [geo_high[c : c + 1], geo_high[c : c + 1], geo_low[c : c + 1], geo_low[c : c + 1]]
    rows.append(jnp.full((1, EH), BLOCKED, bf16))
    rows.append(jnp.zeros((GEO - 13, EH), bf16))
    full_w[pl.ds(0, LAT), :] = send_w[...]
    full_w[pl.ds(LAT, GEO), :] = jnp.concatenate(rows, axis=0)

    for b in range(4):
        a, c = b // 2, b % 2
        codes = codes_ref[a, c]
        window_lat = jnp.concatenate([win[a + w // 3, c + w % 3] for w in range(9)], axis=1)
        if first:
            window_geo = jnp.concatenate([pack[a + w // 3, c + w % 3, 32:48, :] for w in range(9)], axis=1)
            window_lat = jnp.concatenate([window_lat, window_geo], axis=0)
        bound = recv_all[:, b * SLOTS : (b + 1) * SLOTS]
        total = None
        for pair in range(KNB // 2):
            hot = one_hot(codes, pair)
            sender = jnp.dot(window_lat, hot, preferred_element_type=f32)
            if first:
                got = sender[LAT:]
                other_x = got[0:1] + got[1:2] + got[2:3]
                other_y = got[3:4] + got[4:5] + got[5:6]
                own_x = position[a, c, 0:1]
                own_y = position[a, c, 1:2]
                own_live = pack[a + 1, c + 1, 38:39, :].astype(f32)
                twice = lambda v: jnp.concatenate([v, v], axis=1)
                delta_x = other_x - twice(own_x)
                delta_y = other_y - twice(own_y)
                distance = delta_x * delta_x + delta_y * delta_y
                mask = jnp.concatenate([mask_ref[a, c, 2 * pair : 2 * pair + 1], mask_ref[a, c, 2 * pair + 1 : 2 * pair + 2]], axis=1)
                valid = mask.astype(f32) * twice(own_live) * got[6:7]
                pieces = []
                for v in (delta_x, delta_y, distance):
                    v_high = v.astype(bf16).astype(f32)
                    v_low = v - v_high
                    pieces += [v_high, v_low, v_high, v_low]
                pieces.append(1.0 - valid)
                pieces.append(jnp.zeros((GEO - 13, 2 * SLOTS), f32))
                geo = jnp.concatenate(pieces, axis=0).astype(bf16)
                geo_out[b, :, pair * 2 * SLOTS : (pair + 1) * 2 * SLOTS] = geo
                sender = sender[:LAT]
            else:
                geo = geo_in[b, :, pair * 2 * SLOTS : (pair + 1) * 2 * SLOTS]
            right_side = jnp.concatenate([sender.astype(bf16), geo], axis=0)
            hidden = tdot(full_w[...], right_side)
            part = jnp.maximum(hidden[:, :SLOTS], bound) + jnp.maximum(hidden[:, SLOTS:], bound)
            total = part if total is None else total + part
        sums[:, b * SLOTS : (b + 1) * SLOTS] = (total - KNB * bound).astype(bf16)

    summed = tdot(out_w[...], sums[...]).astype(bf16)
    joined = tdot(first_w[...], jnp.concatenate([own_all, summed], axis=0))
    joined = jnp.maximum(joined, 0.0).astype(bf16)
    update = norm_rows(tdot(second_w[...], joined))
    latent = (own_all.astype(f32) + update).astype(bf16)
    if not last:
        for b in range(4):
            out_latent[b // 2, b % 2] = latent[:, b * SLOTS : (b + 1) * SLOTS]
    else:
        hidden = jnp.maximum(tdot(dec_first[...], latent), 0.0).astype(bf16)
        accel = tdot(dec_second[...], hidden)
        lane = lax.broadcasted_iota(jnp.int32, (2, SLOTS), 1)
        for b in range(4):
            a, c = b // 2, b % 2
            live = (lane < occupancy[a, c]).astype(f32)
            speed = velocity[a, c] + time_step * (accel[:, b * SLOTS : (b + 1) * SLOTS] * live)
            out_velocity[a, c] = speed
            out_position[a, c] = position[a, c] + time_step * speed


def shifted(count, by):
    return [(i, i + by) for i in range(count) if 0 <= i + by < count]


def exchange(block):
    slabs, cross = lax.axis_size("slab"), lax.axis_size("cross")
    low = lax.ppermute(block[1:], "slab", shifted(slabs, 1))
    high = lax.ppermute(block[:1], "slab", shifted(slabs, -1))
    first = jnp.concatenate([low[:, :1], block[:, :1], high[:, :1]], axis=0)
    second = jnp.concatenate([low[:, 1:], block[:, 1:], high[:, 1:]], axis=0)
    left = lax.ppermute(second, "cross", shifted(cross, 1))
    right = lax.ppermute(first, "cross", shifted(cross, -1))
    return block, low, high, left, right


def call(first, last, *operands):
    vmem = pl.BlockSpec(memory_space=pltpu.VMEM)
    specs = [vmem] * len(operands)
    if last:
        specs[-5] = pl.BlockSpec(memory_space=pltpu.SMEM)
        out = [jax.ShapeDtypeStruct((2, 2, 2, SLOTS), f32)] * 2
    else:
        out = [jax.ShapeDtypeStruct((2, 2, LAT, SLOTS), bf16)]
    scratch = [
        pltpu.VMEM((4, 4, LAT, SLOTS), bf16),
        pltpu.VMEM((LAT + GEO, EH), bf16),
        pltpu.VMEM((EH, 4 * SLOTS), f32),
        pltpu.VMEM((EH, 4 * SLOTS), bf16),
    ]
    if first:
        out.append(jax.ShapeDtypeStruct((4, GEO, KNB * SLOTS), bf16))
        scratch.insert(0, pltpu.VMEM((4, 4, PACK, SLOTS), bf16))
    return pl.pallas_call(
        functools.partial(step_kernel, first, last),
        out_shape=out,
        in_specs=specs,
        out_specs=[vmem] * len(out),
        scratch_shapes=scratch,
        compiler_params=pltpu.CompilerParams(vmem_limit_bytes=48 << 20),
        name="first_step" if first else "last_step" if last else "middle_step",
    )(*operands)


def shards(
    features,
    position,
    velocity,
    occupancy,
    neighbor_codes,
    edge_mask,
    enc_first,
    enc_second,
    edge_recv,
    edge_send,
    edge_geo,
    edge_out,
    node_first,
    node_second,
    dec_first,
    dec_second,
):
    size_x, size_y = position.shape[:2]
    slot_index = lax.broadcasted_iota(jnp.int32, (size_x, size_y, 1, SLOTS), 3)
    live = (slot_index < occupancy[:, :, None, None]).astype(bf16)
    xs = split3(position[:, :, 0:1])
    ys = split3(position[:, :, 1:2])
    blank = jnp.zeros((size_x, size_y, 2, SLOTS), bf16)
    tail = jnp.zeros((size_x, size_y, PACK - 39, SLOTS), bf16)
    raw = jnp.concatenate([features, blank, *xs, *ys, live, tail], axis=2)
    weights = lambda t: (edge_recv[t], edge_send[t], edge_geo[t], edge_out[t], node_first[t], node_second[t])
    latent, geo = call(True, False, *exchange(raw), neighbor_codes, edge_mask, position, enc_first, enc_second, *weights(0))
    (latent,) = call(False, False, *exchange(latent), neighbor_codes, geo, *weights(1))
    return tuple(
        call(
            False,
            True,
            *exchange(latent),
            neighbor_codes,
            geo,
            *weights(2),
            occupancy,
            position,
            velocity,
            dec_first,
            dec_second,
        )
    )


def solution(mesh):
    tile = P("slab", "cross", None, None)
    return jax.shard_map(
        shards,
        mesh=mesh,
        in_specs=(tile, tile, tile, P("slab", "cross"), tile, tile) + (P(),) * 10,
        out_specs=(tile, tile),
        check_vma=False,
    )
```

```python
import functools

import jax
import jax.numpy as jnp
from jax import lax
from jax.experimental import pallas as pl
from jax.experimental.pallas import tpu as pltpu
from jax.sharding import PartitionSpec as P

time_step = 0.5
LAT = 128
EH = 512
INF = 30
KNB = 16
SLOTS = 128
PACK = 48
GEO = 16
WIDE = 8
BLOCKED = -(2.0**40)
bf16 = jnp.bfloat16
f32 = jnp.float32
i32 = jnp.int32


def tdot(left, right):
    return lax.dot_general(left, right, (((0,), (0,)), ((), ())), preferred_element_type=f32)


def split3(values):
    high = values.astype(bf16).astype(f32)
    rest = values - high
    mid = rest.astype(bf16).astype(f32)
    return [high, mid, rest - mid]


def norm_rows(values):
    center = values - jnp.mean(values, axis=0, keepdims=True)
    spread = jnp.mean(center * center, axis=0, keepdims=True)
    return center * lax.rsqrt(spread + 1e-05)


def parities():
    return lax.rem(lax.axis_index("slab"), 2), lax.rem(lax.axis_index("cross"), 2)


def lane_rows(values, first, count):
    return jnp.concatenate([values[k : k + 1] for k in range(first, first + count)], axis=1)


def repeated(values, count):
    return jnp.concatenate([values] * count, axis=1)


def prepare_kernel(features, position, occupancy, codes, mask, raw, own_codes, send_a, send_b):
    p, q = parities()
    lane = lax.broadcasted_iota(i32, (1, SLOTS), 1)
    for a in range(2):
        for c in range(2):
            live = (lane < occupancy[a, c]).astype(f32)
            rows = [features[a, c].astype(f32), jnp.zeros((2, SLOTS), f32)]
            rows += split3(position[a, c, 0:1]) + split3(position[a, c, 1:2])
            rows += [live, jnp.zeros((PACK - 39, SLOTS), f32)]
            raw[a, c] = jnp.concatenate(rows, axis=0).astype(bf16)
            own_codes[a, c] = jnp.where(mask[a, c] > 0, codes[a, c], (codes[a, c] & (SLOTS - 1)) - SLOTS)
    for near, far, out in ((1 - p, p, send_a), (p, 1 - p, send_b)):
        for c in range(2):
            out[c, 0:PACK] = raw[near, c]
            out[c, PACK : 2 * PACK] = raw[far, c]
            code = own_codes[near, c]
            out[c, 2 * PACK : 2 * PACK + KNB] = (code >> 7).astype(f32).astype(bf16)
            out[c, 2 * PACK + KNB :] = (code & (SLOTS - 1)).astype(f32).astype(bf16)


def pack_raw_kernel(own, got_a, got_b, send_c, send_d):
    p, q = parities()
    for j, out in ((1 - q, send_c), (q, send_d)):
        out[2] = own[0, j]
        out[3] = own[1, j]
        for side, got in ((1 - p, got_a), (p, got_b)):
            out[1 + 3 * side] = got[j, 0:PACK]
            out[5 * side] = got[j, PACK : 2 * PACK]


def pack_kernel(own, got_a, got_b, send_c, send_d):
    p, q = parities()
    for j, out in ((1 - q, send_c), (q, send_d)):
        out[1] = own[0, j]
        out[2] = own[1, j]
        out[3 * (1 - p)] = got_a[j]
        out[3 * p] = got_b[j]


def one_hot(codes):
    wide = codes.shape[1]
    window = codes >> 7
    slot = codes & (SLOTS - 1)
    iota = lax.broadcasted_iota(i32, (SLOTS, wide), 0).astype(jnp.int16)
    parts = []
    for w in range(9):
        wanted = jnp.where(window == w, slot, -1).astype(jnp.int16)
        hit = iota == jnp.broadcast_to(wanted, (SLOTS, wide))
        parts.append(jnp.where(hit, jnp.ones((), bf16), jnp.zeros((), bf16)))
    return jnp.concatenate(parts, axis=0)


def edge_weight(send_w, geo_w, full_w):
    values = geo_w[...]
    high = values.astype(bf16)
    low = (values - high.astype(f32)).astype(bf16)
    rows = []
    for c in range(3):
        rows += [high[c : c + 1], high[c : c + 1], low[c : c + 1], low[c : c + 1]]
    rows.append(jnp.full((1, EH), BLOCKED, bf16))
    rows.append(jnp.zeros((GEO - 13, EH), bf16))
    full_w[0:LAT, :] = send_w[...]
    full_w[LAT:, :] = jnp.concatenate(rows, axis=0)


def geometry_rows(got, own_x, own_y, own_live):
    delta_x = got[0:1] + got[1:2] + got[2:3] - own_x
    delta_y = got[3:4] + got[4:5] + got[5:6] - own_y
    distance = delta_x * delta_x + delta_y * delta_y
    pieces = []
    for v in (delta_x, delta_y, distance):
        high = v.astype(bf16).astype(f32)
        pieces += [high, v - high, high, v - high]
    pieces.append(1.0 - own_live * got[6:7])
    pieces.append(jnp.zeros((GEO - 13, got.shape[1]), f32))
    return jnp.concatenate(pieces, axis=0).astype(bf16)


def edge_sum(full_w, right_side, bound, total):
    hidden = tdot(full_w[...], right_side)
    for k in range(right_side.shape[1] // SLOTS):
        part = jnp.maximum(hidden[:, k * SLOTS : (k + 1) * SLOTS], bound)
        total = part if total is None else total + part
    return total


def node_update(own_all, sums, out_w, first_w, second_w):
    summed = tdot(out_w, sums).astype(bf16)
    joined = tdot(first_w, jnp.concatenate([own_all, summed], axis=0))
    joined = jnp.maximum(joined, 0.0).astype(bf16)
    update = norm_rows(tdot(second_w, joined))
    return (own_all.astype(f32) + update).astype(bf16)


def first_kernel(
    own, got_a, got_b, got_c, got_d, own_codes, enc_first, enc_second, recv_w, send_w, geo_w, out_w, first_w, second_w,
    latent_out, geo_out, send_c, send_d, pack, codes_all, win, own_win, full_w, recv_all, sums,
):
    p, q = parities()
    for c in range(2):
        for a in range(2):
            pack[2 + a, 1 + c] = own[a, c]
            codes_all[1 + a, c] = own_codes[a, c]
        for side, got in ((1 - p, got_a), (p, got_b)):
            pack[1 + 3 * side, 1 + c] = got[c, 0:PACK]
            pack[5 * side, 1 + c] = got[c, PACK : 2 * PACK]
            window = got[c, 2 * PACK : 2 * PACK + KNB].astype(f32)
            slot = got[c, 2 * PACK + KNB :].astype(f32)
            codes_all[3 * side, c] = (window * SLOTS + slot).astype(i32)
    for i in range(6):
        pack[i, 3 * (1 - q)] = got_c[i]
        pack[i, 3 * q] = got_d[i]
    weight = jnp.concatenate([enc_first[...], jnp.zeros((PACK - INF, LAT), bf16)], axis=0)
    for i in range(6):
        raw = jnp.concatenate([pack[i, j] for j in range(4)], axis=1)
        hidden = jnp.maximum(tdot(weight, raw), 0.0).astype(bf16)
        latent = norm_rows(tdot(enc_second[...], hidden)).astype(bf16)
        for j in range(4):
            win[i, j] = latent[:, j * SLOTS : (j + 1) * SLOTS]
    own_all = jnp.concatenate([win[1 + b // 2, 1 + b % 2] for b in range(8)], axis=1)
    recv_all[...] = -tdot(recv_w[0], own_all)
    edge_weight(send_w.at[0], geo_w.at[0], full_w)

    def one_bin(b, carry):
        a, c = lax.div(b, 2), lax.rem(b, 2)
        codes = codes_all[a, c]
        lats = jnp.concatenate([win[a + w // 3, c + w % 3] for w in range(9)], axis=1)
        geos = jnp.concatenate([pack[a + w // 3, c + w % 3, 32:PACK, :] for w in range(9)], axis=1)
        stacked = jnp.concatenate([lats, geos], axis=0)
        me = pack[a + 1, c + 1, 32:PACK, :].astype(f32)
        own_x = repeated(me[0:1] + me[1:2] + me[2:3], WIDE)
        own_y = repeated(me[3:4] + me[4:5] + me[5:6], WIDE)
        own_live = repeated(me[6:7], WIDE)
        columns = pl.ds(pl.multiple_of(b * SLOTS, SLOTS), SLOTS)
        bound = recv_all[:, columns]
        total = None
        for part in range(KNB // WIDE):
            hot = one_hot(lane_rows(codes, part * WIDE, WIDE))
            got = jnp.dot(stacked, hot, preferred_element_type=f32)
            geo = geometry_rows(got[LAT:], own_x, own_y, own_live)
            geo_out[b, :, part * WIDE * SLOTS : (part + 1) * WIDE * SLOTS] = geo
            total = edge_sum(full_w, jnp.concatenate([got[:LAT].astype(bf16), geo], axis=0), bound, total)
        sums[:, columns] = (total - KNB * bound).astype(bf16)
        return carry

    lax.fori_loop(0, 8, one_bin, 0)
    latent = node_update(own_all, sums[...], out_w[0], first_w[0], second_w[0])
    for b in range(8):
        latent_out[b // 2, b % 2] = latent[:, b * SLOTS : (b + 1) * SLOTS]
    for i in range(4):
        send_c[i] = latent_out[i, 1 - q]
        send_d[i] = latent_out[i, q]


def later_step(t, win, own_codes, geo, recv_w, send_w, geo_w, out_w, first_w, second_w, full_w, recv_all, sums):
    own_all = jnp.concatenate([win[1 + b // 2, 1 + b % 2] for b in range(4)], axis=1)
    recv_all[...] = -tdot(recv_w[t], own_all)
    edge_weight(send_w.at[t], geo_w.at[t], full_w)
    for b in range(4):
        a, c = b // 2, b % 2
        codes = own_codes[a, c]
        lats = jnp.concatenate([win[a + w // 3, c + w % 3] for w in range(9)], axis=1)
        bound = recv_all[:, b * SLOTS : (b + 1) * SLOTS]
        total = None
        for part in range(KNB // WIDE):
            hot = one_hot(lane_rows(codes, part * WIDE, WIDE))
            got = jnp.dot(lats, hot, preferred_element_type=f32).astype(bf16)
            rows = geo[2 + b, :, part * WIDE * SLOTS : (part + 1) * WIDE * SLOTS]
            total = edge_sum(full_w, jnp.concatenate([got, rows], axis=0), bound, total)
        sums[:, b * SLOTS : (b + 1) * SLOTS] = (total - KNB * bound).astype(bf16)
    return node_update(own_all, sums[...], out_w[t], first_w[t], second_w[t])


def middle_kernel(
    wide, got_c, got_d, own_codes, geo, recv_w, send_w, geo_w, out_w, first_w, second_w,
    latent_out, send_a, send_b, win, full_w, recv_all, sums,
):
    p, q = parities()
    for i in range(4):
        win[i, 1] = wide[i, 0]
        win[i, 2] = wide[i, 1]
        win[i, 3 * (1 - q)] = got_c[i]
        win[i, 3 * q] = got_d[i]
    latent = later_step(1, win, own_codes, geo, recv_w, send_w, geo_w, out_w, first_w, second_w, full_w, recv_all, sums)
    for b in range(4):
        latent_out[b // 2, b % 2] = latent[:, b * SLOTS : (b + 1) * SLOTS]
    for c in range(2):
        send_a[c] = latent_out[1 - p, c]
        send_b[c] = latent_out[p, c]


def last_kernel(
    own, got_a, got_b, got_c, got_d, own_codes, geo, recv_w, send_w, geo_w, out_w, first_w, second_w,
    occupancy, position, velocity, dec_first, dec_second,
    out_velocity, out_position, win, full_w, recv_all, sums,
):
    p, q = parities()
    for c in range(2):
        win[1, 1 + c] = own[0, c]
        win[2, 1 + c] = own[1, c]
        win[3 * (1 - p), 1 + c] = got_a[c]
        win[3 * p, 1 + c] = got_b[c]
    for i in range(4):
        win[i, 3 * (1 - q)] = got_c[i]
        win[i, 3 * q] = got_d[i]
    latent = later_step(2, win, own_codes, geo, recv_w, send_w, geo_w, out_w, first_w, second_w, full_w, recv_all, sums)
    hidden = jnp.maximum(tdot(dec_first[...], latent), 0.0).astype(bf16)
    accel = tdot(dec_second[...], hidden)
    lane = lax.broadcasted_iota(i32, (2, SLOTS), 1)
    for b in range(4):
        a, c = b // 2, b % 2
        live = (lane < occupancy[a, c]).astype(f32)
        speed = velocity[a, c] + time_step * (accel[:, b * SLOTS : (b + 1) * SLOTS] * live)
        out_velocity[a, c] = speed
        out_position[a, c] = position[a, c] + time_step * speed


def run(kernel, name, out, scratch, operands, scalar=None):
    vmem = pl.BlockSpec(memory_space=pltpu.VMEM)
    specs = [vmem] * len(operands)
    if scalar is not None:
        specs[scalar] = pl.BlockSpec(memory_space=pltpu.SMEM)
    return pl.pallas_call(
        kernel,
        out_shape=[jax.ShapeDtypeStruct(shape, dtype) for shape, dtype in out],
        in_specs=specs,
        out_specs=[vmem] * len(out),
        scratch_shapes=[pltpu.VMEM(shape, dtype) for shape, dtype in scratch],
        compiler_params=pltpu.CompilerParams(vmem_limit_bytes=40 << 20),
        name=name,
    )(*operands)


def swaps(count, start):
    pairs = []
    for low in range(start, count - 1, 2):
        pairs += [(low, low + 1), (low + 1, low)]
    return pairs


def swap(block, axis, start):
    return lax.ppermute(block, axis, swaps(lax.axis_size(axis), start))


def shards(
    features,
    position,
    velocity,
    occupancy,
    neighbor_codes,
    edge_mask,
    enc_first,
    enc_second,
    edge_recv,
    edge_send,
    edge_geo,
    edge_out,
    node_first,
    node_second,
    dec_first,
    dec_second,
):
    weights = (edge_recv, edge_send, edge_geo, edge_out, node_first, node_second)
    tile = (LAT, SLOTS)
    side = ((2, *tile), bf16)
    column = ((4, *tile), bf16)
    raw_column = ((6, PACK, SLOTS), bf16)

    def scratch(bins):
        return [((LAT + GEO, EH), bf16), ((EH, bins * SLOTS), f32), ((EH, bins * SLOTS), bf16)]

    raw, own_codes, send_a, send_b = run(
        prepare_kernel,
        "prepare",
        [((2, 2, PACK, SLOTS), bf16), ((2, 2, KNB, SLOTS), i32), side, side],
        [],
        (features, position, occupancy, neighbor_codes, edge_mask),
        2,
    )
    got_b, got_a = swap(send_b, "slab", 1), swap(send_a, "slab", 0)
    send_c, send_d = run(pack_raw_kernel, "pack_raw", [raw_column] * 2, [], (raw, got_a, got_b))
    got_d, got_c = swap(send_d, "cross", 1), swap(send_c, "cross", 0)
    wide, geo, send_c, send_d = run(
        first_kernel,
        "first_step",
        [((4, 2, *tile), bf16), ((8, GEO, KNB * SLOTS), bf16), column, column],
        [
            ((6, 4, PACK, SLOTS), bf16),
            ((4, 2, KNB, SLOTS), i32),
            ((6, 4, *tile), bf16),
            ((8, *tile), bf16),
            *scratch(8),
        ],
        (raw, got_a, got_b, got_c, got_d, own_codes, enc_first, enc_second, *weights),
    )
    got_d, got_c = swap(send_d, "cross", 1), swap(send_c, "cross", 0)
    latent, send_a, send_b = run(
        middle_kernel,
        "middle_step",
        [((2, 2, *tile), bf16), side, side],
        [((4, 4, *tile), bf16), *scratch(4)],
        (wide, got_c, got_d, own_codes, geo, *weights),
    )
    got_b, got_a = swap(send_b, "slab", 1), swap(send_a, "slab", 0)
    send_c, send_d = run(pack_kernel, "pack", [column] * 2, [], (latent, got_a, got_b))
    got_d, got_c = swap(send_d, "cross", 1), swap(send_c, "cross", 0)
    operands = (latent, got_a, got_b, got_c, got_d, own_codes, geo, *weights)
    return tuple(
        run(
            last_kernel,
            "last_step",
            [((2, 2, 2, SLOTS), f32)] * 2,
            [((4, 4, *tile), bf16), *scratch(4)],
            (*operands, occupancy, position, velocity, dec_first, dec_second),
            len(operands),
        )
    )


def solution(mesh):
    tile = P("slab", "cross", None, None)
    return jax.shard_map(
        shards,
        mesh=mesh,
        in_specs=(tile, tile, tile, P("slab", "cross"), tile, tile) + (P(),) * 10,
        out_specs=(tile, tile),
        check_vma=False,
    )
```

```python
import functools

import jax
import jax.numpy as jnp
from jax import lax
from jax.experimental import pallas as pl
from jax.experimental.pallas import tpu as pltpu
from jax.sharding import PartitionSpec as P

time_step = 0.5
LAT = 128
EH = 512
INF = 30
KNB = 16
SLOTS = 128
PACK = 48
GEO = 16
WIDE = 8
BLOCKED = -(2.0**40)
bf16 = jnp.bfloat16
f32 = jnp.float32
i32 = jnp.int32


def tdot(left, right):
    return lax.dot_general(left, right, (((0,), (0,)), ((), ())), preferred_element_type=f32)


def split3(values):
    high = values.astype(bf16).astype(f32)
    rest = values - high
    mid = rest.astype(bf16).astype(f32)
    return [high, mid, rest - mid]


def norm_rows(values):
    center = values - jnp.mean(values, axis=0, keepdims=True)
    spread = jnp.mean(center * center, axis=0, keepdims=True)
    return center * lax.rsqrt(spread + 1e-05)


def parities():
    return lax.rem(lax.axis_index("slab"), 2), lax.rem(lax.axis_index("cross"), 2)


def lane_rows(values, first, count):
    return jnp.concatenate([values[k : k + 1] for k in range(first, first + count)], axis=1)


def repeated(values, count):
    return jnp.concatenate([values] * count, axis=1)


def prepare_kernel(features_in, position_in, occupancy_in, codes_in, mask_in, raw, own_codes, send_a, send_b,
                   features, position, occupancy, codes, mask, sems):
    pairs = ((features_in, features), (position_in, position), (occupancy_in, occupancy), (codes_in, codes), (mask_in, mask))
    copies = [pltpu.make_async_copy(source, target, sems.at[k]) for k, (source, target) in enumerate(pairs)]
    for copy in copies:
        copy.start()
    p, q = parities()
    lane = lax.broadcasted_iota(i32, (1, SLOTS), 1)
    for copy in copies:
        copy.wait()
    for a in range(2):
        for c in range(2):
            live = (lane < occupancy[a, c]).astype(f32)
            rows = [features[a, c].astype(f32), jnp.zeros((2, SLOTS), f32)]
            rows += split3(position[a, c, 0:1]) + split3(position[a, c, 1:2])
            rows += [live, jnp.zeros((PACK - 39, SLOTS), f32)]
            raw[a, c] = jnp.concatenate(rows, axis=0).astype(bf16)
            own_codes[a, c] = jnp.where(mask[a, c] > 0, codes[a, c], (codes[a, c] & (SLOTS - 1)) - SLOTS)
    for near, far, out in ((1 - p, p, send_a), (p, 1 - p, send_b)):
        for c in range(2):
            out[c, 0:PACK] = raw[near, c]
            out[c, PACK : 2 * PACK] = raw[far, c]
            code = own_codes[near, c]
            out[c, 2 * PACK : 2 * PACK + KNB] = (code >> 7).astype(f32).astype(bf16)
            out[c, 2 * PACK + KNB :] = (code & (SLOTS - 1)).astype(f32).astype(bf16)


def weights_kernel(token, *refs):
    sources, outs, (geo_w, sems) = refs[:9], refs[9:17], refs[17:]
    full_w = outs[0]
    targets = (full_w.at[:, 0:LAT, :], geo_w, *outs[1:])
    copies = [pltpu.make_async_copy(source, target, sems.at[k]) for k, (source, target) in enumerate(zip(sources, targets))]
    for copy in copies:
        copy.start()
    for copy in copies:
        copy.wait()
    for t in range(full_w.shape[0]):
        values = geo_w[t]
        high = values.astype(bf16).astype(f32)
        low = values - high
        rows = []
        for c in range(3):
            rows += [high[c : c + 1], high[c : c + 1], low[c : c + 1], low[c : c + 1]]
        rows.append(jnp.full((1, EH), BLOCKED, f32))
        rows.append(jnp.zeros((GEO - 13, EH), f32))
        full_w[t, LAT:, :] = jnp.concatenate(rows, axis=0).astype(bf16)


def pack_raw_kernel(own, got_a, got_b, send_c, send_d):
    p, q = parities()
    for j, out in ((1 - q, send_c), (q, send_d)):
        out[2] = own[0, j]
        out[3] = own[1, j]
        for side, got in ((1 - p, got_a), (p, got_b)):
            out[1 + 3 * side] = got[j, 0:PACK]
            out[5 * side] = got[j, PACK : 2 * PACK]


def pack_kernel(own, got_a, got_b, send_c, send_d):
    p, q = parities()
    for j, out in ((1 - q, send_c), (q, send_d)):
        out[1] = own[0, j]
        out[2] = own[1, j]
        out[3 * (1 - p)] = got_a[j]
        out[3 * p] = got_b[j]


def one_hot(codes, windows):
    wide = codes.shape[1]
    window = codes >> 7
    slot = codes & (SLOTS - 1)
    iota = lax.broadcasted_iota(i32, (SLOTS, wide), 0).astype(jnp.int16)
    parts = []
    for w in windows:
        wanted = jnp.where(window == w, slot, -1).astype(jnp.int16)
        hit = iota == jnp.broadcast_to(wanted, (SLOTS, wide))
        parts.append(jnp.where(hit, jnp.ones((), bf16), jnp.zeros((), bf16)))
    return jnp.concatenate(parts, axis=0)


def geometry_rows(got, own_x, own_y, own_live):
    delta_x = got[0:1] + got[1:2] + got[2:3] - own_x
    delta_y = got[3:4] + got[4:5] + got[5:6] - own_y
    distance = delta_x * delta_x + delta_y * delta_y
    pieces = []
    for v in (delta_x, delta_y, distance):
        high = v.astype(bf16).astype(f32)
        pieces += [high, v - high, high, v - high]
    pieces.append(1.0 - own_live * got[6:7])
    pieces.append(jnp.zeros((GEO - 13, got.shape[1]), f32))
    return jnp.concatenate(pieces, axis=0).astype(bf16)


def edge_sum(full_w, right_side, bound, total):
    hidden = tdot(full_w, right_side)
    for k in range(right_side.shape[1] // SLOTS):
        part = jnp.maximum(hidden[:, k * SLOTS : (k + 1) * SLOTS], bound)
        total = part if total is None else total + part
    return total


def node_update(own_all, sums, out_w, first_w, second_w):
    summed = tdot(out_w, sums).astype(bf16)
    joined = tdot(first_w, jnp.concatenate([own_all, summed], axis=0))
    joined = jnp.maximum(joined, 0.0).astype(bf16)
    update = norm_rows(tdot(second_w, joined))
    return (own_all.astype(f32) + update).astype(bf16)


def encoded(rows, enc_first, enc_second):
    weight = jnp.concatenate([enc_first[...], jnp.zeros((PACK - INF, LAT), bf16)], axis=0)
    raw = jnp.concatenate(rows, axis=1)
    hidden = jnp.maximum(tdot(weight, raw), 0.0).astype(bf16)
    return norm_rows(tdot(enc_second[...], hidden)).astype(bf16)


def encode_kernel(own, got_a, got_b, own_codes, enc_first, enc_second, recv_w, pack, codes_all, latents, bounds):
    p, q = parities()
    for c in range(2):
        for a in range(2):
            pack[2 + a, c] = own[a, c]
            codes_all[1 + a, c] = own_codes[a, c]
        for side, got in ((1 - p, got_a), (p, got_b)):
            pack[1 + 3 * side, c] = got[c, 0:PACK]
            pack[5 * side, c] = got[c, PACK : 2 * PACK]
            window = got[c, 2 * PACK : 2 * PACK + KNB].astype(f32)
            slot = got[c, 2 * PACK + KNB :].astype(f32)
            codes_all[3 * side, c] = (window * SLOTS + slot).astype(i32)
    for i in range(0, 6, 2):
        latent = encoded([pack[i + j // 2, j % 2] for j in range(4)], enc_first, enc_second)
        for j in range(4):
            latents[i + j // 2, j % 2] = latent[:, j * SLOTS : (j + 1) * SLOTS]
    own_all = jnp.concatenate([latents[1 + b // 2, b % 2] for b in range(8)], axis=1)
    bounds[...] = -tdot(recv_w[0], own_all)


def first_kernel(
    pack_own, codes_all, latents, bounds, got_c, got_d, enc_first, enc_second, full_w, out_w, first_w, second_w,
    latent_out, geo_out, send_c, send_d, pack, win, sums,
):
    p, q = parities()
    for i in range(6):
        for c in range(2):
            pack[i, 1 + c] = pack_own[i, c]
            win[i, 1 + c] = latents[i, c]
        pack[i, 3 * (1 - q)] = got_c[i]
        pack[i, 3 * q] = got_d[i]
    for i in range(0, 6, 2):
        latent = encoded([pack[i + j // 2, 3 * (j % 2)] for j in range(4)], enc_first, enc_second)
        for j in range(4):
            win[i + j // 2, 3 * (j % 2)] = latent[:, j * SLOTS : (j + 1) * SLOTS]

    def one_bin(b, carry):
        a, c = lax.div(b, 2), lax.rem(b, 2)
        codes = codes_all[a, c]
        lats = jnp.concatenate([win[a + w // 3, c + w % 3] for w in range(9)], axis=1)
        geos = jnp.concatenate([pack[a + w // 3, c + w % 3, 32:PACK, :] for w in range(9)], axis=1)
        stacked = jnp.concatenate([lats, geos], axis=0)
        me = pack[a + 1, c + 1, 32:PACK, :].astype(f32)
        own_x = repeated(me[0:1] + me[1:2] + me[2:3], WIDE)
        own_y = repeated(me[3:4] + me[4:5] + me[5:6], WIDE)
        own_live = repeated(me[6:7], WIDE)
        columns = pl.ds(pl.multiple_of(b * SLOTS, SLOTS), SLOTS)
        bound = bounds[:, columns]
        total = None
        for part in range(KNB // WIDE):
            hot = one_hot(lane_rows(codes, part * WIDE, WIDE), range(9))
            got = jnp.dot(stacked, hot, preferred_element_type=f32)
            geo = geometry_rows(got[LAT:], own_x, own_y, own_live)
            geo_out[b, :, part * WIDE * SLOTS : (part + 1) * WIDE * SLOTS] = geo
            total = edge_sum(full_w[0], jnp.concatenate([got[:LAT].astype(bf16), geo], axis=0), bound, total)
        sums[:, columns] = (total - KNB * bound).astype(bf16)
        return carry

    lax.fori_loop(0, 8, one_bin, 0)
    own_all = jnp.concatenate([win[1 + b // 2, 1 + b % 2] for b in range(8)], axis=1)
    latent = node_update(own_all, sums[...], out_w[0], first_w[0], second_w[0])
    for b in range(8):
        latent_out[b // 2, b % 2] = latent[:, b * SLOTS : (b + 1) * SLOTS]
    for i in range(4):
        send_c[i] = latent_out[i, 1 - q]
        send_d[i] = latent_out[i, q]


def inner_windows(c):
    return [w for w in range(9) if c + w % 3 in (1, 2)]


def outer_windows(c):
    return [w for w in range(9) if c + w % 3 in (0, 3)]


def early_part(t, win, own_codes, recv_w, gathered, bounds):
    own_all = jnp.concatenate([win[1 + b // 2, b % 2] for b in range(4)], axis=1)
    bounds[...] = -tdot(recv_w[t], own_all)
    for b in range(4):
        a, c = b // 2, b % 2
        windows = inner_windows(c)
        lats = jnp.concatenate([win[a + w // 3, c + w % 3 - 1] for w in windows], axis=1)
        for part in range(KNB // WIDE):
            hot = one_hot(lane_rows(own_codes[a, c], part * WIDE, WIDE), windows)
            got = jnp.dot(lats, hot, preferred_element_type=f32).astype(bf16)
            gathered[b, :, part * WIDE * SLOTS : (part + 1) * WIDE * SLOTS] = got


def middle_early_kernel(wide, own_codes, recv_w, gathered, bounds):
    early_part(1, wide, own_codes, recv_w, gathered, bounds)


def last_early_kernel(own, got_a, got_b, own_codes, recv_w, gathered, bounds, win):
    p, q = parities()
    for c in range(2):
        win[1, c] = own[0, c]
        win[2, c] = own[1, c]
        win[3 * (1 - p), c] = got_a[c]
        win[3 * p, c] = got_b[c]
    early_part(2, win, own_codes, recv_w, gathered, bounds)


def late_part(t, own_all, got_c, got_d, own_codes, geo, gathered, bounds, full_w, out_w, first_w, second_w, edge, sums):
    p, q = parities()
    for i in range(4):
        edge[1 - q, i] = got_c[i]
        edge[q, i] = got_d[i]
    for b in range(4):
        a, c = b // 2, b % 2
        windows = outer_windows(c)
        lats = jnp.concatenate([edge[c, a + w // 3] for w in windows], axis=1)
        bound = bounds[:, b * SLOTS : (b + 1) * SLOTS]
        total = None
        for part in range(KNB // WIDE):
            columns = slice(part * WIDE * SLOTS, (part + 1) * WIDE * SLOTS)
            hot = one_hot(lane_rows(own_codes[a, c], part * WIDE, WIDE), windows)
            got = jnp.dot(lats, hot, preferred_element_type=f32).astype(bf16) + gathered[b, :, columns]
            total = edge_sum(full_w[t], jnp.concatenate([got, geo[2 + b, :, columns]], axis=0), bound, total)
        sums[:, b * SLOTS : (b + 1) * SLOTS] = (total - KNB * bound).astype(bf16)
    return node_update(own_all, sums[...], out_w[t], first_w[t], second_w[t])


def middle_kernel(
    wide, got_c, got_d, own_codes, geo, gathered, bounds, full_w, out_w, first_w, second_w,
    latent_out, send_a, send_b, edge, sums,
):
    p, q = parities()
    own_all = jnp.concatenate([wide[1 + b // 2, b % 2] for b in range(4)], axis=1)
    latent = late_part(1, own_all, got_c, got_d, own_codes, geo, gathered, bounds, full_w, out_w, first_w, second_w, edge, sums)
    for b in range(4):
        latent_out[b // 2, b % 2] = latent[:, b * SLOTS : (b + 1) * SLOTS]
    for c in range(2):
        send_a[c] = latent_out[1 - p, c]
        send_b[c] = latent_out[p, c]


def last_kernel(
    own, got_c, got_d, own_codes, geo, gathered, bounds, full_w, out_w, first_w, second_w,
    raw, position, velocity, dec_first, dec_second, out_velocity, out_position, edge, sums,
):
    own_all = jnp.concatenate([own[b // 2, b % 2] for b in range(4)], axis=1)
    latent = late_part(2, own_all, got_c, got_d, own_codes, geo, gathered, bounds, full_w, out_w, first_w, second_w, edge, sums)
    hidden = jnp.maximum(tdot(dec_first[...], latent), 0.0).astype(bf16)
    accel = tdot(dec_second[...], hidden)
    for b in range(4):
        a, c = b // 2, b % 2
        live = raw[a, c, 32:PACK].astype(f32)[6:7]
        speed = velocity[a, c] + time_step * (accel[:, b * SLOTS : (b + 1) * SLOTS] * live)
        out_velocity[a, c] = speed
        out_position[a, c] = position[a, c] + time_step * speed


def run(kernel, name, out, scratch, operands, outside=(), work=None):
    vmem = pl.BlockSpec(memory_space=pltpu.VMEM)
    far = pl.BlockSpec(memory_space=pltpu.HBM)
    operands = [
        pltpu.with_memory_space_constraint(x, pltpu.HBM) if k in outside else x for k, x in enumerate(operands)
    ]
    return pl.pallas_call(
        kernel,
        out_shape=[jax.ShapeDtypeStruct(shape, dtype) for shape, dtype in out],
        in_specs=[far if k in outside else vmem for k in range(len(operands))],
        out_specs=[vmem] * len(out),
        scratch_shapes=[pltpu.VMEM(*entry) if isinstance(entry, tuple) else entry for entry in scratch],
        compiler_params=pltpu.CompilerParams(vmem_limit_bytes=32 << 20),
        cost_estimate=None if work is None else pl.CostEstimate(flops=work, bytes_accessed=4 << 20, transcendentals=0),
        name=name,
    )(*operands)


def swaps(count, start):
    pairs = []
    for low in range(start, count - 1, 2):
        pairs += [(low, low + 1), (low + 1, low)]
    return pairs


def swap(block, axis, start):
    return lax.ppermute(block, axis, swaps(lax.axis_size(axis), start))


def shards(
    features,
    position,
    velocity,
    occupancy,
    neighbor_codes,
    edge_mask,
    enc_first,
    enc_second,
    edge_recv,
    edge_send,
    edge_geo,
    edge_out,
    node_first,
    node_second,
    dec_first,
    dec_second,
):
    tile = (LAT, SLOTS)
    side = ((2, *tile), bf16)
    column = ((4, *tile), bf16)
    raw_column = ((6, PACK, SLOTS), bf16)
    steps = edge_recv.shape[0]
    whole = lambda values: (values.shape, values.dtype)
    gathered = ((4, LAT, KNB * SLOTS), bf16)
    bounds = ((EH, 4 * SLOTS), f32)

    inputs = (features, position, occupancy, neighbor_codes, edge_mask)
    raw, own_codes, send_a, send_b = run(
        prepare_kernel,
        "prepare",
        [((2, 2, PACK, SLOTS), bf16), ((2, 2, KNB, SLOTS), i32), side, side],
        [
            whole(features),
            whole(position),
            pltpu.SMEM(occupancy.shape, i32),
            whole(neighbor_codes),
            whole(edge_mask),
            pltpu.SemaphoreType.DMA((5,)),
        ],
        inputs,
        range(5),
    )
    got_b, got_a = swap(send_b, "slab", 1), swap(send_a, "slab", 0)
    plain = (edge_recv, edge_out, node_first, node_second, enc_first, enc_second, dec_first)
    full_w, recv_w, out_w, first_w, second_w, enc_one, enc_two, dec_one = run(
        weights_kernel,
        "weights",
        [((steps, LAT + GEO, EH), bf16), *[whole(w) for w in plain]],
        [whole(edge_geo), pltpu.SemaphoreType.DMA((9,))],
        (own_codes, edge_send, edge_geo, *plain),
        range(1, 10),
        1 << 30,
    )
    send_c, send_d = run(pack_raw_kernel, "pack_raw", [raw_column] * 2, [], (raw, got_a, got_b))
    got_d, got_c = swap(send_d, "cross", 1), swap(send_c, "cross", 0)
    pack_own, codes_all, latents, all_bounds = run(
        encode_kernel,
        "encode",
        [((6, 2, PACK, SLOTS), bf16), ((4, 2, KNB, SLOTS), i32), ((6, 2, *tile), bf16), ((EH, 8 * SLOTS), f32)],
        [],
        (raw, got_a, got_b, own_codes, enc_one, enc_two, recv_w),
        (),
        1 << 30,
    )
    wide, geo, send_c, send_d = run(
        first_kernel,
        "first_step",
        [((4, 2, *tile), bf16), ((8, GEO, KNB * SLOTS), bf16), column, column],
        [((6, 4, PACK, SLOTS), bf16), ((6, 4, *tile), bf16), ((EH, 8 * SLOTS), bf16)],
        (pack_own, codes_all, latents, all_bounds, got_c, got_d, enc_one, enc_two, full_w, out_w, first_w, second_w),
    )
    got_d, got_c = swap(send_d, "cross", 1), swap(send_c, "cross", 0)
    part, bound = run(middle_early_kernel, "middle_early", [gathered, bounds], [], (wide, own_codes, recv_w), (), 1 << 31)
    late = [((2, *column[0]), bf16), ((EH, 4 * SLOTS), bf16)]
    latent, send_a, send_b = run(
        middle_kernel,
        "middle_step",
        [((2, 2, *tile), bf16), side, side],
        late,
        (wide, got_c, got_d, own_codes, geo, part, bound, full_w, out_w, first_w, second_w),
    )
    got_b, got_a = swap(send_b, "slab", 1), swap(send_a, "slab", 0)
    send_c, send_d = run(pack_kernel, "pack", [column] * 2, [], (latent, got_a, got_b))
    got_d, got_c = swap(send_d, "cross", 1), swap(send_c, "cross", 0)
    part, bound = run(
        last_early_kernel,
        "last_early",
        [gathered, bounds],
        [((4, 2, *tile), bf16)],
        (latent, got_a, got_b, own_codes, recv_w),
        (),
        1 << 31,
    )
    operands = (latent, got_c, got_d, own_codes, geo, part, bound, full_w, out_w, first_w, second_w)
    return tuple(
        run(
            last_kernel,
            "last_step",
            [((2, 2, 2, SLOTS), f32)] * 2,
            late,
            (*operands, raw, position, velocity, dec_one, dec_second),
        )
    )


def solution(mesh):
    tile = P("slab", "cross", None, None)
    return jax.shard_map(
        shards,
        mesh=mesh,
        in_specs=(tile, tile, tile, P("slab", "cross"), tile, tile) + (P(),) * 10,
        out_specs=(tile, tile),
        check_vma=False,
    )
```

```python
import functools

import jax
import jax.numpy as jnp
from jax import lax
from jax.experimental import pallas as pl
from jax.experimental.pallas import tpu as pltpu
from jax.sharding import PartitionSpec as P

time_step = 0.5
LAT = 128
EH = 512
INF = 30
KNB = 16
SLOTS = 128
PACK = 48
GEO = 16
WIDE = 8
BLOCKED = -(2.0**40)
bf16 = jnp.bfloat16
f32 = jnp.float32
i32 = jnp.int32


def tdot(left, right):
    return lax.dot_general(left, right, (((0,), (0,)), ((), ())), preferred_element_type=f32)


def split3(values):
    high = values.astype(bf16).astype(f32)
    rest = values - high
    mid = rest.astype(bf16).astype(f32)
    return [high, mid, rest - mid]


def norm_rows(values):
    center = values - jnp.mean(values, axis=0, keepdims=True)
    spread = jnp.mean(center * center, axis=0, keepdims=True)
    return center * lax.rsqrt(spread + 1e-05)


def parities():
    return lax.rem(lax.axis_index("slab"), 2), lax.rem(lax.axis_index("cross"), 2)


def lane_rows(values, first, count):
    return jnp.concatenate([values[k : k + 1] for k in range(first, first + count)], axis=1)


def repeated(values, count):
    return jnp.concatenate([values] * count, axis=1)


def prepare_kernel(features_in, position_in, occupancy_in, codes_in, mask_in, raw, own_codes, send_a, send_b,
                   features, position, occupancy, codes, mask, sems):
    pairs = ((features_in, features), (position_in, position), (occupancy_in, occupancy), (codes_in, codes), (mask_in, mask))
    copies = [pltpu.make_async_copy(source, target, sems.at[k]) for k, (source, target) in enumerate(pairs)]
    for copy in copies:
        copy.start()
    p, q = parities()
    lane = lax.broadcasted_iota(i32, (1, SLOTS), 1)
    for copy in copies:
        copy.wait()
    for a in range(2):
        for c in range(2):
            live = (lane < occupancy[a, c]).astype(f32)
            rows = [features[a, :, c, :].astype(f32), jnp.zeros((2, SLOTS), f32)]
            rows += split3(position[a, c, 0:1]) + split3(position[a, c, 1:2])
            rows += [live, jnp.zeros((PACK - 39, SLOTS), f32)]
            raw[a, c] = jnp.concatenate(rows, axis=0).astype(bf16)
            own_codes[a, c] = jnp.where(mask[a, c] > 0, codes[a, c], (codes[a, c] & (SLOTS - 1)) - SLOTS)
    for near, far, out in ((1 - p, p, send_a), (p, 1 - p, send_b)):
        for c in range(2):
            out[c, 0:PACK] = raw[near, c]
            out[c, PACK : 2 * PACK] = raw[far, c]
            code = own_codes[near, c]
            out[c, 2 * PACK : 2 * PACK + KNB] = (code >> 7).astype(f32).astype(bf16)
            out[c, 2 * PACK + KNB :] = (code & (SLOTS - 1)).astype(f32).astype(bf16)


def weights_kernel(token, *refs):
    sources, outs, (geo_w, sems) = refs[:9], refs[9:17], refs[17:]
    full_w = outs[0]
    targets = (full_w.at[:, 0:LAT, :], geo_w, *outs[1:])
    copies = [pltpu.make_async_copy(source, target, sems.at[k]) for k, (source, target) in enumerate(zip(sources, targets))]
    for copy in copies:
        copy.start()
    for copy in copies:
        copy.wait()
    for t in range(full_w.shape[0]):
        values = geo_w[t]
        high = values.astype(bf16).astype(f32)
        low = values - high
        rows = []
        for c in range(3):
            rows += [high[c : c + 1], high[c : c + 1], low[c : c + 1], low[c : c + 1]]
        rows.append(jnp.full((1, EH), BLOCKED, f32))
        rows.append(jnp.zeros((GEO - 13, EH), f32))
        full_w[t, LAT:, :] = jnp.concatenate(rows, axis=0).astype(bf16)


def pack_raw_kernel(own, got_a, got_b, token, send_c, send_d):
    p, q = parities()
    for j, out in ((1 - q, send_c), (q, send_d)):
        out[2] = own[0, j]
        out[3] = own[1, j]
        for side, got in ((1 - p, got_a), (p, got_b)):
            out[1 + 3 * side] = got[j, 0:PACK]
            out[5 * side] = got[j, PACK : 2 * PACK]


def pack_kernel(own, got_a, got_b, send_c, send_d):
    p, q = parities()
    for j, out in ((1 - q, send_c), (q, send_d)):
        out[1] = own[0, j]
        out[2] = own[1, j]
        out[3 * (1 - p)] = got_a[j]
        out[3 * p] = got_b[j]


def one_hot(window, slot, numbers):
    wide = slot.shape[1]
    iota = lax.broadcasted_iota(i32, (SLOTS, wide), 0).astype(jnp.int16)
    parts = []
    for number in numbers:
        wanted = jnp.where(window == number, slot, -1).astype(jnp.int16)
        hit = iota == jnp.broadcast_to(wanted, (SLOTS, wide))
        parts.append(jnp.where(hit, jnp.ones((), bf16), jnp.zeros((), bf16)))
    return jnp.concatenate(parts, axis=0)


def pick(codes, tiles, direct):
    window = codes >> 7
    slot = codes & (SLOTS - 1)
    hot = one_hot(window, slot, [number for number, _ in tiles])
    got = jnp.dot(jnp.concatenate([tile for _, tile in tiles], axis=1), hot, preferred_element_type=f32)
    if direct is None:
        return got
    number, tile = direct
    tile = tile.astype(f32)
    parts = []
    for k in range(codes.shape[1] // SLOTS):
        lanes = slice(k * SLOTS, (k + 1) * SLOTS)
        index = jnp.broadcast_to(slot[:, lanes], tile.shape)
        here = jnp.broadcast_to(window[:, lanes], tile.shape) == number
        moved = jnp.take_along_axis(tile, index, axis=1, mode="promise_in_bounds")
        parts.append(jnp.where(here, moved, got[:, lanes]))
    return jnp.concatenate(parts, axis=1)


def inner_tiles(s, a, tile_of):
    return [(3 * d + 1 - s + j, tile_of(a + d, j)) for d in range(3) for j in range(2)]


def outer_tiles(s, a, tile_of):
    return [(3 * d + 2 * s, tile_of(a + d)) for d in range(3)]


def geometry_rows(got, own_x, own_y, own_live):
    delta_x = got[0:1] + got[1:2] + got[2:3] - own_x
    delta_y = got[3:4] + got[4:5] + got[5:6] - own_y
    distance = delta_x * delta_x + delta_y * delta_y
    pieces = []
    for v in (delta_x, delta_y, distance):
        high = v.astype(bf16).astype(f32)
        pieces += [high, v - high, high, v - high]
    pieces.append(1.0 - own_live * got[6:7])
    pieces.append(jnp.zeros((GEO - 13, got.shape[1]), f32))
    return jnp.concatenate(pieces, axis=0).astype(bf16)


def edge_sum(full_w, right_side, bound, total):
    hidden = tdot(full_w, right_side)
    for k in range(right_side.shape[1] // SLOTS):
        part = jnp.maximum(hidden[:, k * SLOTS : (k + 1) * SLOTS], bound)
        total = part if total is None else total + part
    return total


def node_update(own_all, sums, out_w, first_w, second_w):
    summed = tdot(out_w, sums).astype(bf16)
    joined = tdot(first_w, jnp.concatenate([own_all, summed], axis=0))
    joined = jnp.maximum(joined, 0.0).astype(bf16)
    update = norm_rows(tdot(second_w, joined))
    return (own_all.astype(f32) + update).astype(bf16)


def encoded(rows, enc_first, enc_second):
    weight = jnp.concatenate([enc_first[...], jnp.zeros((PACK - INF, LAT), bf16)], axis=0)
    raw = jnp.concatenate(rows, axis=1)
    hidden = jnp.maximum(tdot(weight, raw), 0.0).astype(bf16)
    return norm_rows(tdot(enc_second[...], hidden)).astype(bf16)


def first_bins(s, inner, pack_inner, outer, pack_outer, codes_all, bounds, full_w, sums, geo_out):
    def inner_tile(i, j):
        return jnp.concatenate([inner[i, j], pack_inner[i, j, 32:PACK, :]], axis=0)

    def outer_tile(i):
        return jnp.concatenate([outer[i], pack_outer[i, 32:PACK, :]], axis=0)

    def one_bin(a, carry):
        codes = codes_all[a, s]
        tiles = outer_tiles(s, a, outer_tile) + inner_tiles(s, a, inner_tile)
        me = pack_inner[a + 1, s, 32:PACK, :].astype(f32)
        own_x = repeated(me[0:1] + me[1:2] + me[2:3], WIDE)
        own_y = repeated(me[3:4] + me[4:5] + me[5:6], WIDE)
        own_live = repeated(me[6:7], WIDE)
        columns = pl.ds(pl.multiple_of(a * SLOTS, SLOTS), SLOTS)
        bound = bounds[:, columns]
        total = None
        for part in range(KNB // WIDE):
            got = pick(lane_rows(codes, part * WIDE, WIDE), tiles[:-1], tiles[-1])
            geo = geometry_rows(got[LAT:], own_x, own_y, own_live)
            geo_out[a, :, part * WIDE * SLOTS : (part + 1) * WIDE * SLOTS] = geo
            total = edge_sum(full_w[0], jnp.concatenate([got[:LAT].astype(bf16), geo], axis=0), bound, total)
        sums[:, columns] = (total - KNB * bound).astype(bf16)
        return carry

    lax.fori_loop(0, 4, one_bin, 0)


def first_early_kernel(
    own, got_a, got_b, got_c, own_codes, enc_first, enc_second, recv_w, full_w,
    pack, codes_all, inner, bounds_d, sums_c, geo_c, outer, bounds_c,
):
    p, q = parities()
    for c in range(2):
        for a in range(2):
            pack[2 + a, c] = own[a, c]
            codes_all[1 + a, c] = own_codes[a, c]
        for side, got in ((1 - p, got_a), (p, got_b)):
            pack[1 + 3 * side, c] = got[c, 0:PACK]
            pack[5 * side, c] = got[c, PACK : 2 * PACK]
            window = got[c, 2 * PACK : 2 * PACK + KNB].astype(f32)
            slot = got[c, 2 * PACK + KNB :].astype(f32)
            codes_all[3 * side, c] = (window * SLOTS + slot).astype(i32)
    for i in range(0, 6, 2):
        rows = [pack[i + j // 2, j % 2] for j in range(4)] + [got_c[i], got_c[i + 1]]
        latent = encoded(rows, enc_first, enc_second)
        for j in range(4):
            inner[i + j // 2, j % 2] = latent[:, j * SLOTS : (j + 1) * SLOTS]
        for j in range(2):
            outer[i + j] = latent[:, (4 + j) * SLOTS : (5 + j) * SLOTS]
    for s, bounds in ((1 - q, bounds_c), (q, bounds_d)):
        bounds[...] = -tdot(recv_w[0], jnp.concatenate([inner[1 + a, s] for a in range(4)], axis=1))
    first_bins(1 - q, inner, pack, outer, got_c, codes_all, bounds_c, full_w, sums_c, geo_c)


def first_kernel(
    pack, codes_all, inner, bounds_d, sums_c, got_d, enc_first, enc_second, full_w, out_w, first_w, second_w,
    latent_out, geo_d, send_c, send_d, outer, sums_d,
):
    p, q = parities()
    latent = encoded([got_d[i] for i in range(6)], enc_first, enc_second)
    for i in range(6):
        outer[i] = latent[:, i * SLOTS : (i + 1) * SLOTS]
    first_bins(q, inner, pack, outer, got_d, codes_all, bounds_d, full_w, sums_d, geo_d)
    own_all = jnp.concatenate([inner[1 + a, s] for s in (1 - q, q) for a in range(4)], axis=1)
    sums = jnp.concatenate([sums_c[...], sums_d[...]], axis=1)
    latent = node_update(own_all, sums, out_w[0], first_w[0], second_w[0])
    for i in range(4):
        for s, send, at in ((1 - q, send_c, i), (q, send_d, 4 + i)):
            tile = latent[:, at * SLOTS : (at + 1) * SLOTS]
            send[i] = tile
            latent_out[i, s] = tile


def early_part(t, inner, got_c, own_codes, geo_c, recv_w, full_w, sums_c, gathered_d, bounds_d):
    p, q = parities()
    outs = [-tdot(recv_w[t], jnp.concatenate([inner[1, s], inner[2, s]], axis=1)) for s in (1 - q, q)]
    bounds_d[...] = outs[1]
    for a in range(2):
        bound = outs[0][:, a * SLOTS : (a + 1) * SLOTS]
        tiles = outer_tiles(1 - q, a, lambda i: got_c[i]) + inner_tiles(1 - q, a, lambda i, j: inner[i, j])
        total = None
        for part in range(KNB // WIDE):
            columns = slice(part * WIDE * SLOTS, (part + 1) * WIDE * SLOTS)
            got = pick(lane_rows(own_codes[a, 1 - q], part * WIDE, WIDE), tiles[:-1], tiles[-1]).astype(bf16)
            total = edge_sum(full_w[t], jnp.concatenate([got, geo_c[1 + a, :, columns]], axis=0), bound, total)
        sums_c[:, a * SLOTS : (a + 1) * SLOTS] = (total - KNB * bound).astype(bf16)
    for a in range(2):
        tiles = inner_tiles(q, a, lambda i, j: inner[i, j])
        for part in range(KNB // WIDE):
            columns = slice(part * WIDE * SLOTS, (part + 1) * WIDE * SLOTS)
            gathered_d[a, :, columns] = pick(lane_rows(own_codes[a, q], part * WIDE, WIDE), tiles, None).astype(bf16)


def middle_early_kernel(wide, got_c, own_codes, geo_c, recv_w, full_w, sums_c, gathered_d, bounds_d):
    early_part(1, wide, got_c, own_codes, geo_c, recv_w, full_w, sums_c, gathered_d, bounds_d)


def last_early_kernel(own, got_a, got_b, got_c, own_codes, geo_c, recv_w, full_w, sums_c, gathered_d, bounds_d, inner):
    p, q = parities()
    for c in range(2):
        inner[1, c] = own[0, c]
        inner[2, c] = own[1, c]
        inner[3 * (1 - p), c] = got_a[c]
        inner[3 * p, c] = got_b[c]
    early_part(2, inner, got_c, own_codes, geo_c, recv_w, full_w, sums_c, gathered_d, bounds_d)


def late_part(t, own_all, got_d, own_codes, geo_d, sums_c, gathered_d, bounds_d, full_w, out_w, first_w, second_w):
    p, q = parities()
    sums = [sums_c[...]]
    for a in range(2):
        tiles = outer_tiles(q, a, lambda i: got_d[i])
        bound = bounds_d[:, a * SLOTS : (a + 1) * SLOTS]
        total = None
        for part in range(KNB // WIDE):
            columns = slice(part * WIDE * SLOTS, (part + 1) * WIDE * SLOTS)
            got = pick(lane_rows(own_codes[a, q], part * WIDE, WIDE), tiles[:-1], tiles[-1]).astype(bf16)
            rows = jnp.concatenate([got + gathered_d[a, :, columns], geo_d[1 + a, :, columns]], axis=0)
            total = edge_sum(full_w[t], rows, bound, total)
        sums.append((total - KNB * bound).astype(bf16))
    return node_update(own_all, jnp.concatenate(sums, axis=1), out_w[t], first_w[t], second_w[t])


def middle_kernel(
    wide, got_d, own_codes, geo_d, sums_c, gathered_d, bounds_d, full_w, out_w, first_w, second_w,
    latent_out, send_a, send_b,
):
    p, q = parities()
    own_all = jnp.concatenate([wide[1 + a, s] for s in (1 - q, q) for a in range(2)], axis=1)
    latent = late_part(1, own_all, got_d, own_codes, geo_d, sums_c, gathered_d, bounds_d, full_w, out_w, first_w, second_w)
    for a in range(2):
        latent_out[a, 1 - q] = latent[:, a * SLOTS : (a + 1) * SLOTS]
        latent_out[a, q] = latent[:, (2 + a) * SLOTS : (3 + a) * SLOTS]
    for c in range(2):
        send_a[c] = latent_out[1 - p, c]
        send_b[c] = latent_out[p, c]


def last_kernel(
    own, got_d, own_codes, geo_d, sums_c, gathered_d, bounds_d, full_w, out_w, first_w, second_w,
    raw, position, velocity, dec_first, dec_second, out_velocity, out_position,
):
    p, q = parities()
    own_all = jnp.concatenate([own[a, s] for s in (1 - q, q) for a in range(2)], axis=1)
    latent = late_part(2, own_all, got_d, own_codes, geo_d, sums_c, gathered_d, bounds_d, full_w, out_w, first_w, second_w)
    hidden = jnp.maximum(tdot(dec_first[...], latent), 0.0).astype(bf16)
    accel = tdot(dec_second[...], hidden)
    for b in range(4):
        a, c = b % 2, (1 - q, q)[b // 2]
        live = raw[a, c, 32:PACK].astype(f32)[6:7]
        speed = velocity[a, c] + time_step * (accel[:, b * SLOTS : (b + 1) * SLOTS] * live)
        out_velocity[a, c] = speed
        out_position[a, c] = position[a, c] + time_step * speed


def run(kernel, name, out, scratch, operands, outside=(), work=None):
    vmem = pl.BlockSpec(memory_space=pltpu.VMEM)
    far = pl.BlockSpec(memory_space=pltpu.HBM)
    operands = [
        pltpu.with_memory_space_constraint(x, pltpu.HBM) if k in outside else x for k, x in enumerate(operands)
    ]
    return pl.pallas_call(
        kernel,
        out_shape=[jax.ShapeDtypeStruct(shape, dtype) for shape, dtype in out],
        in_specs=[far if k in outside else vmem for k in range(len(operands))],
        out_specs=[vmem] * len(out),
        scratch_shapes=[pltpu.VMEM(*entry) if isinstance(entry, tuple) else entry for entry in scratch],
        compiler_params=pltpu.CompilerParams(vmem_limit_bytes=32 << 20),
        cost_estimate=None if work is None else pl.CostEstimate(flops=work, bytes_accessed=4 << 20, transcendentals=0),
        name=name,
    )(*operands)


def swaps(count, start):
    pairs = []
    for low in range(start, count - 1, 2):
        pairs += [(low, low + 1), (low + 1, low)]
    return pairs


def swap(block, axis, start):
    return lax.ppermute(block, axis, swaps(lax.axis_size(axis), start))


def shards(
    features,
    position,
    velocity,
    occupancy,
    neighbor_codes,
    edge_mask,
    enc_first,
    enc_second,
    edge_recv,
    edge_send,
    edge_geo,
    edge_out,
    node_first,
    node_second,
    dec_first,
    dec_second,
):
    tile = (LAT, SLOTS)
    side = ((2, *tile), bf16)
    column = ((4, *tile), bf16)
    raw_column = ((6, PACK, SLOTS), bf16)
    steps = edge_recv.shape[0]
    whole = lambda values: (values.shape, values.dtype)
    geometry = ((4, GEO, KNB * SLOTS), bf16)
    early = [((EH, 2 * SLOTS), bf16), ((2, LAT, KNB * SLOTS), bf16), ((EH, 2 * SLOTS), f32)]

    features = jnp.transpose(features, (0, 2, 1, 3))
    inputs = (features, position, occupancy, neighbor_codes, edge_mask)
    raw, own_codes, send_a, send_b = run(
        prepare_kernel,
        "prepare",
        [((2, 2, PACK, SLOTS), bf16), ((2, 2, KNB, SLOTS), i32), side, side],
        [
            whole(features),
            whole(position),
            pltpu.SMEM(occupancy.shape, i32),
            whole(neighbor_codes),
            whole(edge_mask),
            pltpu.SemaphoreType.DMA((5,)),
        ],
        inputs,
        range(5),
    )
    got_b, got_a = swap(send_b, "slab", 1), swap(send_a, "slab", 0)
    plain = (edge_recv, edge_out, node_first, node_second, enc_first, enc_second, dec_first)
    full_w, recv_w, out_w, first_w, second_w, enc_one, enc_two, dec_one = run(
        weights_kernel,
        "weights",
        [((steps, LAT + GEO, EH), bf16), *[whole(w) for w in plain]],
        [whole(edge_geo), pltpu.SemaphoreType.DMA((9,))],
        (own_codes, edge_send, edge_geo, *plain),
        range(1, 10),
        1 << 30,
    )
    send_c, send_d = run(pack_raw_kernel, "pack_raw", [raw_column] * 2, [], (raw, got_a, got_b, enc_one))
    got_d, got_c = swap(send_d, "cross", 1), swap(send_c, "cross", 0)
    pack, codes_all, inner, bounds_d, sums_c, geo_c = run(
        first_early_kernel,
        "first_early",
        [
            ((6, 2, PACK, SLOTS), bf16),
            ((4, 2, KNB, SLOTS), i32),
            ((6, 2, *tile), bf16),
            ((EH, 4 * SLOTS), f32),
            ((EH, 4 * SLOTS), bf16),
            geometry,
        ],
        [((6, *tile), bf16), ((EH, 4 * SLOTS), f32)],
        (raw, got_a, got_b, got_c, own_codes, enc_one, enc_two, recv_w, full_w),
        (),
        1 << 31,
    )
    wide, geo_d, send_c, send_d = run(
        first_kernel,
        "first_step",
        [((4, 2, *tile), bf16), geometry, column, column],
        [((6, *tile), bf16), ((EH, 4 * SLOTS), bf16)],
        (pack, codes_all, inner, bounds_d, sums_c, got_d, enc_one, enc_two, full_w, out_w, first_w, second_w),
    )
    got_d, got_c = swap(send_d, "cross", 1), swap(send_c, "cross", 0)
    parts = run(
        middle_early_kernel, "middle_early", early, [], (wide, got_c, own_codes, geo_c, recv_w, full_w), (), 1 << 31
    )
    latent, send_a, send_b = run(
        middle_kernel,
        "middle_step",
        [((2, 2, *tile), bf16), side, side],
        [],
        (wide, got_d, own_codes, geo_d, *parts, full_w, out_w, first_w, second_w),
    )
    got_b, got_a = swap(send_b, "slab", 1), swap(send_a, "slab", 0)
    send_c, send_d = run(pack_kernel, "pack", [column] * 2, [], (latent, got_a, got_b))
    got_d, got_c = swap(send_d, "cross", 1), swap(send_c, "cross", 0)
    parts = run(
        last_early_kernel,
        "last_early",
        early,
        [((4, 2, *tile), bf16)],
        (latent, got_a, got_b, got_c, own_codes, geo_c, recv_w, full_w),
        (),
        1 << 31,
    )
    operands = (latent, got_d, own_codes, geo_d, *parts, full_w, out_w, first_w, second_w)
    return tuple(
        run(
            last_kernel,
            "last_step",
            [((2, 2, 2, SLOTS), f32)] * 2,
            [],
            (*operands, raw, position, velocity, dec_one, dec_second),
        )
    )


def solution(mesh):
    tile = P("slab", "cross", None, None)
    return jax.shard_map(
        shards,
        mesh=mesh,
        in_specs=(tile, tile, tile, P("slab", "cross"), tile, tile) + (P(),) * 10,
        out_specs=(tile, tile),
        check_vma=False,
    )
```

```python
import functools

import jax
import jax.numpy as jnp
from jax import lax
from jax.experimental import pallas as pl
from jax.experimental.pallas import tpu as pltpu
from jax.sharding import PartitionSpec as P

time_step = 0.5
LAT = 128
EH = 512
INF = 30
KNB = 16
SLOTS = 128
PACK = 48
GEO = 16
WIDE = 8
UNROLL = 4
BLOCKED = -(2.0**40)
bf16 = jnp.bfloat16
f32 = jnp.float32
i32 = jnp.int32


def tdot(left, right):
    return lax.dot_general(left, right, (((0,), (0,)), ((), ())), preferred_element_type=f32)


def split3(values):
    high = values.astype(bf16).astype(f32)
    rest = values - high
    mid = rest.astype(bf16).astype(f32)
    return [high, mid, rest - mid]


def norm_rows(values):
    center = values - jnp.mean(values, axis=0, keepdims=True)
    spread = jnp.mean(center * center, axis=0, keepdims=True)
    return center * lax.rsqrt(spread + 1e-05)


def parities():
    return lax.rem(lax.axis_index("slab"), 2), lax.rem(lax.axis_index("cross"), 2)


def lane_rows(values, first, count):
    return jnp.concatenate([values[k : k + 1] for k in range(first, first + count)], axis=1)


def repeated(values, count):
    return jnp.concatenate([values] * count, axis=1)


def prepare_kernel(features_in, position_in, occupancy_in, codes_in, mask_in, raw, own_codes, send_a, send_b,
                   features, position, occupancy, codes, mask, sems):
    pairs = ((features_in, features), (position_in, position), (occupancy_in, occupancy), (codes_in, codes), (mask_in, mask))
    copies = [pltpu.make_async_copy(source, target, sems.at[k]) for k, (source, target) in enumerate(pairs)]
    for copy in copies:
        copy.start()
    p, q = parities()
    lane = lax.broadcasted_iota(i32, (1, SLOTS), 1)
    for copy in copies:
        copy.wait()
    for a in range(2):
        for c in range(2):
            live = (lane < occupancy[a, c]).astype(f32)
            rows = [features[a, :, c, :].astype(f32), jnp.zeros((2, SLOTS), f32)]
            rows += split3(position[a, c, 0:1]) + split3(position[a, c, 1:2])
            rows += [live, jnp.zeros((PACK - 39, SLOTS), f32)]
            raw[a, c] = jnp.concatenate(rows, axis=0).astype(bf16)
            own_codes[a, c] = jnp.where(mask[a, c] > 0, codes[a, c], (codes[a, c] & (SLOTS - 1)) - SLOTS)
    for near, far, out in ((1 - p, p, send_a), (p, 1 - p, send_b)):
        for c in range(2):
            out[c, 0:PACK] = raw[near, c]
            out[c, PACK : 2 * PACK] = raw[far, c]
            code = own_codes[near, c]
            out[c, 2 * PACK : 2 * PACK + KNB] = (code >> 7).astype(f32).astype(bf16)
            out[c, 2 * PACK + KNB :] = (code & (SLOTS - 1)).astype(f32).astype(bf16)


def weights_kernel(token, *refs):
    count = len(refs) // 2
    sources, outs, (geo_w, sems) = refs[:count], refs[count:-2], refs[-2:]
    full_w = outs[0]
    targets = (full_w.at[:, 0:LAT, :], geo_w, *outs[1:])
    copies = [pltpu.make_async_copy(source, target, sems.at[k]) for k, (source, target) in enumerate(zip(sources, targets))]
    for copy in copies:
        copy.start()
    for copy in copies:
        copy.wait()
    for t in range(full_w.shape[0]):
        values = geo_w[t]
        high = values.astype(bf16).astype(f32)
        low = values - high
        rows = []
        for c in range(3):
            rows += [high[c : c + 1], high[c : c + 1], low[c : c + 1], low[c : c + 1]]
        rows.append(jnp.full((1, EH), BLOCKED, f32))
        rows.append(jnp.zeros((GEO - 13, EH), f32))
        full_w[t, LAT:, :] = jnp.concatenate(rows, axis=0).astype(bf16)


def pack_raw_kernel(own, got_a, got_b, token, send_c, send_d):
    p, q = parities()
    for j, out in ((1 - q, send_c), (q, send_d)):
        out[2] = own[0, j]
        out[3] = own[1, j]
        for side, got in ((1 - p, got_a), (p, got_b)):
            out[1 + 3 * side] = got[j, 0:PACK]
            out[5 * side] = got[j, PACK : 2 * PACK]


def pack_kernel(own, got_a, got_b, send_c, send_d):
    p, q = parities()
    for j, out in ((1 - q, send_c), (q, send_d)):
        out[1] = own[0, j]
        out[2] = own[1, j]
        out[3 * (1 - p)] = got_a[j]
        out[3 * p] = got_b[j]


def one_hot(window, slot, numbers):
    wide = slot.shape[1]
    iota = lax.broadcasted_iota(i32, (SLOTS, wide), 0).astype(jnp.int16)
    parts = []
    for number in numbers:
        wanted = jnp.where(window == number, slot, -1).astype(jnp.int16)
        hit = iota == jnp.broadcast_to(wanted, (SLOTS, wide))
        parts.append(jnp.where(hit, jnp.ones((), bf16), jnp.zeros((), bf16)))
    return jnp.concatenate(parts, axis=0)


def pick(codes, tiles, direct):
    window = codes >> 7
    slot = codes & (SLOTS - 1)
    hot = one_hot(window, slot, [number for number, _ in tiles])
    got = jnp.dot(jnp.concatenate([tile for _, tile in tiles], axis=1), hot, preferred_element_type=f32)
    parts = []
    for k in range(codes.shape[1] // SLOTS):
        lanes = slice(k * SLOTS, (k + 1) * SLOTS)
        part = got[:, lanes]
        index = jnp.broadcast_to(slot[:, lanes], part.shape)
        for number, tile in direct:
            here = jnp.broadcast_to(window[:, lanes], part.shape) == number
            moved = jnp.take_along_axis(tile.astype(f32), index, axis=1, mode="promise_in_bounds")
            part = jnp.where(here, moved, part)
        parts.append(part)
    return jnp.concatenate(parts, axis=1)


def inner_tiles(s, a, tile_of):
    return [(3 * d + 1 - s + j, tile_of(a + d, j)) for d in range(3) for j in range(2)]


def outer_tiles(s, a, tile_of):
    return [(3 * d + 2 * s, tile_of(a + d)) for d in range(3)]


def geometry_rows(got, own_x, own_y, own_live):
    delta_x = got[0:1] + got[1:2] + got[2:3] - own_x
    delta_y = got[3:4] + got[4:5] + got[5:6] - own_y
    distance = delta_x * delta_x + delta_y * delta_y
    pieces = []
    for v in (delta_x, delta_y, distance):
        high = v.astype(bf16).astype(f32)
        pieces += [high, v - high, high, v - high]
    pieces.append(1.0 - own_live * got[6:7])
    pieces.append(jnp.zeros((GEO - 13, got.shape[1]), f32))
    return jnp.concatenate(pieces, axis=0).astype(bf16)


def edge_sum(full_w, right_side, bound, total):
    hidden = tdot(full_w, right_side)
    for k in range(right_side.shape[1] // SLOTS):
        part = jnp.maximum(hidden[:, k * SLOTS : (k + 1) * SLOTS], bound)
        total = part if total is None else total + part
    return total


def node_update(own_all, sums, out_w, first_w, second_w):
    summed = tdot(out_w, sums).astype(bf16)
    joined = tdot(first_w, jnp.concatenate([own_all, summed], axis=0))
    joined = jnp.maximum(joined, 0.0).astype(bf16)
    update = norm_rows(tdot(second_w, joined))
    return (own_all.astype(f32) + update).astype(bf16)


def encoded(rows, enc_first, enc_second):
    weight = jnp.concatenate([enc_first[...], jnp.zeros((PACK - INF, LAT), bf16)], axis=0)
    raw = jnp.concatenate(rows, axis=1)
    hidden = jnp.maximum(tdot(weight, raw), 0.0).astype(bf16)
    return norm_rows(tdot(enc_second[...], hidden)).astype(bf16)


def first_bins(s, inner, pack_inner, outer, pack_outer, codes_all, bounds, full_w, sums, geo_out):
    def inner_tile(i, j):
        return jnp.concatenate([inner[i, j], pack_inner[i, j, 32:PACK, :]], axis=0)

    def outer_tile(i):
        return jnp.concatenate([outer[i], pack_outer[i, 32:PACK, :]], axis=0)

    def one_bin(a, carry):
        codes = codes_all[a, s]
        tiles = outer_tiles(s, a, outer_tile) + inner_tiles(s, a, inner_tile)
        me = pack_inner[a + 1, s, 32:PACK, :].astype(f32)
        own_x = repeated(me[0:1] + me[1:2] + me[2:3], WIDE)
        own_y = repeated(me[3:4] + me[4:5] + me[5:6], WIDE)
        own_live = repeated(me[6:7], WIDE)
        columns = pl.ds(pl.multiple_of(a * SLOTS, SLOTS), SLOTS)
        bound = bounds[:, columns]
        total = None
        for part in range(KNB // WIDE):
            got = pick(lane_rows(codes, part * WIDE, WIDE), tiles[:-1], tiles[-1:])
            geo = geometry_rows(got[LAT:], own_x, own_y, own_live)
            geo_out[a, :, part * WIDE * SLOTS : (part + 1) * WIDE * SLOTS] = geo
            total = edge_sum(full_w[0], jnp.concatenate([got[:LAT].astype(bf16), geo], axis=0), bound, total)
        sums[:, columns] = (total - KNB * bound).astype(bf16)
        return carry

    lax.fori_loop(0, 4, one_bin, 0, unroll=UNROLL)


def first_early_kernel(
    own, got_a, got_b, got_c, own_codes, enc_first, enc_second, recv_w, full_w,
    pack, codes_all, inner, bounds_d, sums_c, geo_c, outer, bounds_c,
):
    p, q = parities()
    for c in range(2):
        for a in range(2):
            pack[2 + a, c] = own[a, c]
            codes_all[1 + a, c] = own_codes[a, c]
        for side, got in ((1 - p, got_a), (p, got_b)):
            pack[1 + 3 * side, c] = got[c, 0:PACK]
            pack[5 * side, c] = got[c, PACK : 2 * PACK]
            window = got[c, 2 * PACK : 2 * PACK + KNB].astype(f32)
            slot = got[c, 2 * PACK + KNB :].astype(f32)
            codes_all[3 * side, c] = (window * SLOTS + slot).astype(i32)
    for i in range(0, 6, 2):
        rows = [pack[i + j // 2, j % 2] for j in range(4)] + [got_c[i], got_c[i + 1]]
        latent = encoded(rows, enc_first, enc_second)
        for j in range(4):
            inner[i + j // 2, j % 2] = latent[:, j * SLOTS : (j + 1) * SLOTS]
        for j in range(2):
            outer[i + j] = latent[:, (4 + j) * SLOTS : (5 + j) * SLOTS]
    for s, bounds in ((1 - q, bounds_c), (q, bounds_d)):
        bounds[...] = -tdot(recv_w[0], jnp.concatenate([inner[1 + a, s] for a in range(4)], axis=1))
    first_bins(1 - q, inner, pack, outer, got_c, codes_all, bounds_c, full_w, sums_c, geo_c)


def first_kernel(
    pack, codes_all, inner, bounds_d, sums_c, got_d, enc_first, enc_second, full_w, out_w, first_w, second_w,
    latent_out, geo_d, send_c, send_d, outer, sums_d,
):
    p, q = parities()
    latent = encoded([got_d[i] for i in range(6)], enc_first, enc_second)
    for i in range(6):
        outer[i] = latent[:, i * SLOTS : (i + 1) * SLOTS]
    first_bins(q, inner, pack, outer, got_d, codes_all, bounds_d, full_w, sums_d, geo_d)
    own_all = jnp.concatenate([inner[1 + a, s] for s in (1 - q, q) for a in range(4)], axis=1)
    sums = jnp.concatenate([sums_c[...], sums_d[...]], axis=1)
    latent = node_update(own_all, sums, out_w[0], first_w[0], second_w[0])
    for i in range(4):
        for s, send, at in ((1 - q, send_c, i), (q, send_d, 4 + i)):
            tile = latent[:, at * SLOTS : (at + 1) * SLOTS]
            send[i] = tile
            latent_out[i, s] = tile


def early_part(t, inner, got_c, own_codes, geo_c, recv_w, full_w, sums_c, gathered_d, bounds_d):
    p, q = parities()
    outs = [-tdot(recv_w[t], jnp.concatenate([inner[1, s], inner[2, s]], axis=1)) for s in (1 - q, q)]
    bounds_d[...] = outs[1]
    for a in range(2):
        bound = outs[0][:, a * SLOTS : (a + 1) * SLOTS]
        tiles = outer_tiles(1 - q, a, lambda i: got_c[i]) + inner_tiles(1 - q, a, lambda i, j: inner[i, j])
        total = None
        for part in range(KNB // WIDE):
            columns = slice(part * WIDE * SLOTS, (part + 1) * WIDE * SLOTS)
            got = pick(lane_rows(own_codes[a, 1 - q], part * WIDE, WIDE), tiles[:-1], tiles[-1:]).astype(bf16)
            total = edge_sum(full_w[t], jnp.concatenate([got, geo_c[1 + a, :, columns]], axis=0), bound, total)
        sums_c[:, a * SLOTS : (a + 1) * SLOTS] = (total - KNB * bound).astype(bf16)
    for a in range(2):
        tiles = inner_tiles(q, a, lambda i, j: inner[i, j])
        for part in range(KNB // WIDE):
            columns = slice(part * WIDE * SLOTS, (part + 1) * WIDE * SLOTS)
            gathered_d[a, :, columns] = pick(lane_rows(own_codes[a, q], part * WIDE, WIDE), tiles, []).astype(bf16)


def middle_early_kernel(wide, got_c, own_codes, geo_c, recv_w, full_w, sums_c, gathered_d, bounds_d):
    early_part(1, wide, got_c, own_codes, geo_c, recv_w, full_w, sums_c, gathered_d, bounds_d)


def last_early_kernel(own, got_a, got_b, got_c, own_codes, geo_c, recv_w, full_w, sums_c, gathered_d, bounds_d, inner):
    p, q = parities()
    for c in range(2):
        inner[1, c] = own[0, c]
        inner[2, c] = own[1, c]
        inner[3 * (1 - p), c] = got_a[c]
        inner[3 * p, c] = got_b[c]
    early_part(2, inner, got_c, own_codes, geo_c, recv_w, full_w, sums_c, gathered_d, bounds_d)


def late_part(t, own_all, got_d, own_codes, geo_d, sums_c, gathered_d, bounds_d, full_w, out_w, first_w, second_w):
    p, q = parities()
    sums = [sums_c[...]]
    for a in range(2):
        tiles = outer_tiles(q, a, lambda i: got_d[i])
        bound = bounds_d[:, a * SLOTS : (a + 1) * SLOTS]
        total = None
        for part in range(KNB // WIDE):
            columns = slice(part * WIDE * SLOTS, (part + 1) * WIDE * SLOTS)
            got = pick(lane_rows(own_codes[a, q], part * WIDE, WIDE), tiles[:-1], tiles[-1:]).astype(bf16)
            rows = jnp.concatenate([got + gathered_d[a, :, columns], geo_d[1 + a, :, columns]], axis=0)
            total = edge_sum(full_w[t], rows, bound, total)
        sums.append((total - KNB * bound).astype(bf16))
    return node_update(own_all, jnp.concatenate(sums, axis=1), out_w[t], first_w[t], second_w[t])


def middle_kernel(
    wide, got_d, own_codes, geo_d, sums_c, gathered_d, bounds_d, full_w, out_w, first_w, second_w,
    latent_out, send_a, send_b,
):
    p, q = parities()
    own_all = jnp.concatenate([wide[1 + a, s] for s in (1 - q, q) for a in range(2)], axis=1)
    latent = late_part(1, own_all, got_d, own_codes, geo_d, sums_c, gathered_d, bounds_d, full_w, out_w, first_w, second_w)
    for a in range(2):
        latent_out[a, 1 - q] = latent[:, a * SLOTS : (a + 1) * SLOTS]
        latent_out[a, q] = latent[:, (2 + a) * SLOTS : (3 + a) * SLOTS]
    for c in range(2):
        send_a[c] = latent_out[1 - p, c]
        send_b[c] = latent_out[p, c]


def last_kernel(
    own, got_d, own_codes, geo_d, sums_c, gathered_d, bounds_d, full_w, out_w, first_w, second_w,
    raw, position, velocity, dec_first, dec_second, out_velocity, out_position,
):
    p, q = parities()
    own_all = jnp.concatenate([own[a, s] for s in (1 - q, q) for a in range(2)], axis=1)
    latent = late_part(2, own_all, got_d, own_codes, geo_d, sums_c, gathered_d, bounds_d, full_w, out_w, first_w, second_w)
    hidden = jnp.maximum(tdot(dec_first[...], latent), 0.0).astype(bf16)
    accel = jnp.dot(dec_second[...], hidden, preferred_element_type=f32)
    for b in range(4):
        a, c = b % 2, (1 - q, q)[b // 2]
        live = raw[a, c, 32:PACK].astype(f32)[6:7]
        speed = velocity[a, c] + time_step * (accel[:, b * SLOTS : (b + 1) * SLOTS] * live)
        out_velocity[a, c] = speed
        out_position[a, c] = position[a, c] + time_step * speed


def run(kernel, name, out, scratch, operands, outside=(), work=None):
    vmem = pl.BlockSpec(memory_space=pltpu.VMEM)
    far = pl.BlockSpec(memory_space=pltpu.HBM)
    operands = [
        pltpu.with_memory_space_constraint(x, pltpu.HBM) if k in outside else x for k, x in enumerate(operands)
    ]
    return pl.pallas_call(
        kernel,
        out_shape=[jax.ShapeDtypeStruct(shape, dtype) for shape, dtype in out],
        in_specs=[far if k in outside else vmem for k in range(len(operands))],
        out_specs=[vmem] * len(out),
        scratch_shapes=[pltpu.VMEM(*entry) if isinstance(entry, tuple) else entry for entry in scratch],
        compiler_params=pltpu.CompilerParams(vmem_limit_bytes=32 << 20),
        cost_estimate=None if work is None else pl.CostEstimate(flops=work, bytes_accessed=4 << 20, transcendentals=0),
        name=name,
    )(*operands)


def swaps(count, start):
    pairs = []
    for low in range(start, count - 1, 2):
        pairs += [(low, low + 1), (low + 1, low)]
    return pairs


def swap(block, axis, start):
    return lax.ppermute(block, axis, swaps(lax.axis_size(axis), start))


def shards(
    features,
    position,
    velocity,
    occupancy,
    neighbor_codes,
    edge_mask,
    enc_first,
    enc_second,
    edge_recv,
    edge_send,
    edge_geo,
    edge_out,
    node_first,
    node_second,
    dec_first,
    dec_second,
):
    tile = (LAT, SLOTS)
    side = ((2, *tile), bf16)
    column = ((4, *tile), bf16)
    raw_column = ((6, PACK, SLOTS), bf16)
    steps = edge_recv.shape[0]
    whole = lambda values: (values.shape, values.dtype)
    geometry = ((4, GEO, KNB * SLOTS), bf16)
    early = [((EH, 2 * SLOTS), bf16), ((2, LAT, KNB * SLOTS), bf16), ((EH, 2 * SLOTS), f32)]

    features = jnp.transpose(features, (0, 2, 1, 3))
    inputs = (features, position, occupancy, neighbor_codes, edge_mask)
    raw, own_codes, send_a, send_b = run(
        prepare_kernel,
        "prepare",
        [((2, 2, PACK, SLOTS), bf16), ((2, 2, KNB, SLOTS), i32), side, side],
        [
            whole(features),
            whole(position),
            pltpu.SMEM(occupancy.shape, i32),
            whole(neighbor_codes),
            whole(edge_mask),
            pltpu.SemaphoreType.DMA((5,)),
        ],
        inputs,
        range(5),
    )
    got_a, got_b = swap(send_a, "slab", 0), swap(send_b, "slab", 1)
    plain = (
        edge_recv, edge_out, node_first, node_second, enc_first, enc_second, dec_first, dec_second.T, position, velocity
    )
    full_w, recv_w, out_w, first_w, second_w, enc_one, enc_two, dec_one, dec_two, place, speed = run(
        weights_kernel,
        "weights",
        [((steps, LAT + GEO, EH), bf16), *[whole(w) for w in plain]],
        [whole(edge_geo), pltpu.SemaphoreType.DMA((2 + len(plain),))],
        (own_codes, edge_send, edge_geo, *plain),
        range(1, 3 + len(plain)),
        1 << 30,
    )
    send_c, send_d = run(pack_raw_kernel, "pack_raw", [raw_column] * 2, [], (raw, got_a, got_b, enc_one))
    got_d, got_c = swap(send_d, "cross", 1), swap(send_c, "cross", 0)
    pack, codes_all, inner, bounds_d, sums_c, geo_c = run(
        first_early_kernel,
        "first_early",
        [
            ((6, 2, PACK, SLOTS), bf16),
            ((4, 2, KNB, SLOTS), i32),
            ((6, 2, *tile), bf16),
            ((EH, 4 * SLOTS), f32),
            ((EH, 4 * SLOTS), bf16),
            geometry,
        ],
        [((6, *tile), bf16), ((EH, 4 * SLOTS), f32)],
        (raw, got_a, got_b, got_c, own_codes, enc_one, enc_two, recv_w, full_w),
        (),
        1 << 31,
    )
    wide, geo_d, send_c, send_d = run(
        first_kernel,
        "first_step",
        [((4, 2, *tile), bf16), geometry, column, column],
        [((6, *tile), bf16), ((EH, 4 * SLOTS), bf16)],
        (pack, codes_all, inner, bounds_d, sums_c, got_d, enc_one, enc_two, full_w, out_w, first_w, second_w),
    )
    got_d, got_c = swap(send_d, "cross", 1), swap(send_c, "cross", 0)
    parts = run(
        middle_early_kernel, "middle_early", early, [], (wide, got_c, own_codes, geo_c, recv_w, full_w), (), 1 << 31
    )
    latent, send_a, send_b = run(
        middle_kernel,
        "middle_step",
        [((2, 2, *tile), bf16), side, side],
        [],
        (wide, got_d, own_codes, geo_d, *parts, full_w, out_w, first_w, second_w),
    )
    got_a, got_b = swap(send_a, "slab", 0), swap(send_b, "slab", 1)
    send_c, send_d = run(pack_kernel, "pack", [column] * 2, [], (latent, got_a, got_b))
    got_d, got_c = swap(send_d, "cross", 1), swap(send_c, "cross", 0)
    parts = run(
        last_early_kernel,
        "last_early",
        early,
        [((4, 2, *tile), bf16)],
        (latent, got_a, got_b, got_c, own_codes, geo_c, recv_w, full_w),
        (),
        1 << 31,
    )
    operands = (latent, got_d, own_codes, geo_d, *parts, full_w, out_w, first_w, second_w)
    return tuple(
        run(
            last_kernel,
            "last_step",
            [((2, 2, 2, SLOTS), f32)] * 2,
            [],
            (*operands, raw, place, speed, dec_one, dec_two),
        )
    )


def solution(mesh):
    tile = P("slab", "cross", None, None)
    return jax.shard_map(
        shards,
        mesh=mesh,
        in_specs=(tile, tile, tile, P("slab", "cross"), tile, tile) + (P(),) * 10,
        out_specs=(tile, tile),
        check_vma=False,
    )
```

```python
import functools

import jax
import jax.numpy as jnp
from jax import lax
from jax.experimental import pallas as pl
from jax.experimental.pallas import tpu as pltpu
from jax.sharding import PartitionSpec as P

time_step = 0.5
LAT = 128
EH = 512
INF = 30
KNB = 16
SLOTS = 128
PACK = 48
GEO = 16
WIDE = 8
UNROLL = 4
BLOCKED = -(2.0**40)
bf16 = jnp.bfloat16
f32 = jnp.float32
i32 = jnp.int32


def tdot(left, right):
    return lax.dot_general(left, right, (((0,), (0,)), ((), ())), preferred_element_type=f32)


def split3(values):
    high = values.astype(bf16).astype(f32)
    rest = values - high
    mid = rest.astype(bf16).astype(f32)
    return [high, mid, rest - mid]


def norm_rows(values):
    center = values - jnp.mean(values, axis=0, keepdims=True)
    spread = jnp.mean(center * center, axis=0, keepdims=True)
    return center * lax.rsqrt(spread + 1e-05)


def parities():
    return lax.rem(lax.axis_index("slab"), 2), lax.rem(lax.axis_index("cross"), 2)


def lane_rows(values, first, count):
    return jnp.concatenate([values[k : k + 1] for k in range(first, first + count)], axis=1)


def repeated(values, count):
    return jnp.concatenate([values] * count, axis=1)


def prepare_kernel(features, position_in, occupancy_in, codes_in, mask_in, raw, own_codes, send_a, send_b,
                   position, occupancy, codes, mask, sems):
    pairs = ((position_in, position), (occupancy_in, occupancy), (codes_in, codes), (mask_in, mask))
    copies = [pltpu.make_async_copy(source, target, sems.at[k]) for k, (source, target) in enumerate(pairs)]
    for copy in copies:
        copy.start()
    p, q = parities()
    lane = lax.broadcasted_iota(i32, (1, SLOTS), 1)
    for copy in copies:
        copy.wait()
    for a in range(2):
        for c in range(2):
            live = (lane < occupancy[a, c]).astype(f32)
            rows = [features[a, :, c, :].astype(f32), jnp.zeros((2, SLOTS), f32)]
            rows += split3(position[a, c, 0:1]) + split3(position[a, c, 1:2])
            rows += [live, jnp.zeros((PACK - 39, SLOTS), f32)]
            raw[a, c] = jnp.concatenate(rows, axis=0).astype(bf16)
            own_codes[a, c] = jnp.where(mask[a, c] > 0, codes[a, c], (codes[a, c] & (SLOTS - 1)) - SLOTS)
    for near, far, out in ((1 - p, p, send_a), (p, 1 - p, send_b)):
        for c in range(2):
            out[c, 0:PACK] = raw[near, c]
            out[c, PACK : 2 * PACK] = raw[far, c]
            code = own_codes[near, c]
            out[c, 2 * PACK : 2 * PACK + KNB] = (code >> 7).astype(f32).astype(bf16)
            out[c, 2 * PACK + KNB :] = (code & (SLOTS - 1)).astype(f32).astype(bf16)


def weights_kernel(token, *refs):
    count = len(refs) // 2
    sources, outs, (geo_w, sems) = refs[:count], refs[count:-2], refs[-2:]
    full_w = outs[0]
    targets = (full_w.at[:, 0:LAT, :], geo_w, *outs[1:])
    copies = [pltpu.make_async_copy(source, target, sems.at[k]) for k, (source, target) in enumerate(zip(sources, targets))]
    for copy in copies:
        copy.start()
    for copy in copies:
        copy.wait()
    for t in range(full_w.shape[0]):
        values = geo_w[t]
        high = values.astype(bf16).astype(f32)
        low = values - high
        rows = []
        for c in range(3):
            rows += [high[c : c + 1], high[c : c + 1], low[c : c + 1], low[c : c + 1]]
        rows.append(jnp.full((1, EH), BLOCKED, f32))
        rows.append(jnp.zeros((GEO - 13, EH), f32))
        full_w[t, LAT:, :] = jnp.concatenate(rows, axis=0).astype(bf16)


def pack_raw_kernel(own, got_a, got_b, token, send_c, send_d):
    p, q = parities()
    for j, out in ((1 - q, send_c), (q, send_d)):
        out[2] = own[0, j]
        out[3] = own[1, j]
        for side, got in ((1 - p, got_a), (p, got_b)):
            out[1 + 3 * side] = got[j, 0:PACK]
            out[5 * side] = got[j, PACK : 2 * PACK]


def pack_kernel(own, got_a, got_b, send_c, send_d):
    p, q = parities()
    for j, out in ((1 - q, send_c), (q, send_d)):
        out[1] = own[0, j]
        out[2] = own[1, j]
        out[3 * (1 - p)] = got_a[j]
        out[3 * p] = got_b[j]


def one_hot(window, slot, numbers):
    wide = slot.shape[1]
    iota = lax.broadcasted_iota(i32, (SLOTS, wide), 0).astype(jnp.int16)
    parts = []
    for number in numbers:
        wanted = jnp.where(window == number, slot, -1).astype(jnp.int16)
        hit = iota == jnp.broadcast_to(wanted, (SLOTS, wide))
        parts.append(jnp.where(hit, jnp.ones((), bf16), jnp.zeros((), bf16)))
    return jnp.concatenate(parts, axis=0)


def pick(codes, tiles, direct):
    window = codes >> 7
    slot = codes & (SLOTS - 1)
    hot = one_hot(window, slot, [number for number, _ in tiles])
    got = jnp.dot(jnp.concatenate([tile for _, tile in tiles], axis=1), hot, preferred_element_type=f32)
    parts = []
    for k in range(codes.shape[1] // SLOTS):
        lanes = slice(k * SLOTS, (k + 1) * SLOTS)
        part = got[:, lanes]
        index = jnp.broadcast_to(slot[:, lanes], part.shape)
        for number, tile in direct:
            here = jnp.broadcast_to(window[:, lanes], part.shape) == number
            moved = jnp.take_along_axis(tile.astype(f32), index, axis=1, mode="promise_in_bounds")
            part = jnp.where(here, moved, part)
        parts.append(part)
    return jnp.concatenate(parts, axis=1)


def inner_tiles(s, a, tile_of):
    return [(3 * d + 1 - s + j, tile_of(a + d, j)) for d in range(3) for j in range(2)]


def outer_tiles(s, a, tile_of):
    return [(3 * d + 2 * s, tile_of(a + d)) for d in range(3)]


def geometry_rows(got, own_x, own_y, own_live):
    delta_x = got[0:1] + got[1:2] + got[2:3] - own_x
    delta_y = got[3:4] + got[4:5] + got[5:6] - own_y
    distance = delta_x * delta_x + delta_y * delta_y
    pieces = []
    for v in (delta_x, delta_y, distance):
        high = v.astype(bf16).astype(f32)
        pieces += [high, v - high, high, v - high]
    pieces.append(1.0 - own_live * got[6:7])
    pieces.append(jnp.zeros((GEO - 13, got.shape[1]), f32))
    return jnp.concatenate(pieces, axis=0).astype(bf16)


def edge_sum(full_w, right_side, bound, total):
    hidden = tdot(full_w, right_side)
    for k in range(right_side.shape[1] // SLOTS):
        part = jnp.maximum(hidden[:, k * SLOTS : (k + 1) * SLOTS], bound)
        total = part if total is None else total + part
    return total


def node_update(own_all, sums, out_w, first_w, second_w):
    summed = tdot(out_w, sums).astype(bf16)
    joined = tdot(first_w, jnp.concatenate([own_all, summed], axis=0))
    joined = jnp.maximum(joined, 0.0).astype(bf16)
    update = norm_rows(tdot(second_w, joined))
    return (own_all.astype(f32) + update).astype(bf16)


def encoded(rows, enc_first, enc_second):
    weight = jnp.concatenate([enc_first[...], jnp.zeros((PACK - INF, LAT), bf16)], axis=0)
    raw = jnp.concatenate(rows, axis=1)
    hidden = jnp.maximum(tdot(weight, raw), 0.0).astype(bf16)
    return norm_rows(tdot(enc_second[...], hidden)).astype(bf16)


def first_bins(s, inner, pack_inner, outer, pack_outer, codes_all, bounds, full_w, sums, geo_out):
    def inner_tile(i, j):
        return jnp.concatenate([inner[i, j], pack_inner[i, j, 32:PACK, :]], axis=0)

    def outer_tile(i):
        return jnp.concatenate([outer[i], pack_outer[i, 32:PACK, :]], axis=0)

    def one_bin(a, carry):
        codes = codes_all[a, s]
        tiles = outer_tiles(s, a, outer_tile) + inner_tiles(s, a, inner_tile)
        me = pack_inner[a + 1, s, 32:PACK, :].astype(f32)
        own_x = repeated(me[0:1] + me[1:2] + me[2:3], WIDE)
        own_y = repeated(me[3:4] + me[4:5] + me[5:6], WIDE)
        own_live = repeated(me[6:7], WIDE)
        columns = pl.ds(pl.multiple_of(a * SLOTS, SLOTS), SLOTS)
        bound = bounds[:, columns]
        total = None
        for part in range(KNB // WIDE):
            got = pick(lane_rows(codes, part * WIDE, WIDE), tiles[:-1], tiles[-1:])
            geo = geometry_rows(got[LAT:], own_x, own_y, own_live)
            geo_out[a, :, part * WIDE * SLOTS : (part + 1) * WIDE * SLOTS] = geo
            total = edge_sum(full_w[0], jnp.concatenate([got[:LAT].astype(bf16), geo], axis=0), bound, total)
        sums[:, columns] = (total - KNB * bound).astype(bf16)
        return carry

    lax.fori_loop(0, 4, one_bin, 0, unroll=UNROLL)


def first_early_kernel(
    own, got_a, got_b, got_c, own_codes, enc_first, enc_second, recv_w, full_w,
    pack, codes_all, inner, bounds_d, sums_c, geo_c, outer, bounds_c,
):
    p, q = parities()
    for c in range(2):
        for a in range(2):
            pack[2 + a, c] = own[a, c]
            codes_all[1 + a, c] = own_codes[a, c]
        for side, got in ((1 - p, got_a), (p, got_b)):
            pack[1 + 3 * side, c] = got[c, 0:PACK]
            pack[5 * side, c] = got[c, PACK : 2 * PACK]
            window = got[c, 2 * PACK : 2 * PACK + KNB].astype(f32)
            slot = got[c, 2 * PACK + KNB :].astype(f32)
            codes_all[3 * side, c] = (window * SLOTS + slot).astype(i32)
    for i in range(0, 6, 2):
        rows = [pack[i + j // 2, j % 2] for j in range(4)] + [got_c[i], got_c[i + 1]]
        latent = encoded(rows, enc_first, enc_second)
        for j in range(4):
            inner[i + j // 2, j % 2] = latent[:, j * SLOTS : (j + 1) * SLOTS]
        for j in range(2):
            outer[i + j] = latent[:, (4 + j) * SLOTS : (5 + j) * SLOTS]
    for s, bounds in ((1 - q, bounds_c), (q, bounds_d)):
        bounds[...] = -tdot(recv_w[0], jnp.concatenate([inner[1 + a, s] for a in range(4)], axis=1))
    first_bins(1 - q, inner, pack, outer, got_c, codes_all, bounds_c, full_w, sums_c, geo_c)


def first_kernel(
    pack, codes_all, inner, bounds_d, sums_c, got_d, enc_first, enc_second, full_w, out_w, first_w, second_w,
    latent_out, geo_d, send_c, send_d, outer, sums_d,
):
    p, q = parities()
    latent = encoded([got_d[i] for i in range(6)], enc_first, enc_second)
    for i in range(6):
        outer[i] = latent[:, i * SLOTS : (i + 1) * SLOTS]
    first_bins(q, inner, pack, outer, got_d, codes_all, bounds_d, full_w, sums_d, geo_d)
    own_all = jnp.concatenate([inner[1 + a, s] for s in (1 - q, q) for a in range(4)], axis=1)
    sums = jnp.concatenate([sums_c[...], sums_d[...]], axis=1)
    latent = node_update(own_all, sums, out_w[0], first_w[0], second_w[0])
    for i in range(4):
        for s, send, at in ((1 - q, send_c, i), (q, send_d, 4 + i)):
            tile = latent[:, at * SLOTS : (at + 1) * SLOTS]
            send[i] = tile
            latent_out[i, s] = tile


def early_part(t, inner, got_c, own_codes, geo_c, recv_w, full_w, sums_c, gathered_d, bounds_d):
    p, q = parities()
    outs = [-tdot(recv_w[t], jnp.concatenate([inner[1, s], inner[2, s]], axis=1)) for s in (1 - q, q)]
    bounds_d[...] = outs[1]
    for a in range(2):
        bound = outs[0][:, a * SLOTS : (a + 1) * SLOTS]
        tiles = outer_tiles(1 - q, a, lambda i: got_c[i]) + inner_tiles(1 - q, a, lambda i, j: inner[i, j])
        total = None
        for part in range(KNB // WIDE):
            columns = slice(part * WIDE * SLOTS, (part + 1) * WIDE * SLOTS)
            got = pick(lane_rows(own_codes[a, 1 - q], part * WIDE, WIDE), tiles[:-1], tiles[-1:]).astype(bf16)
            total = edge_sum(full_w[t], jnp.concatenate([got, geo_c[1 + a, :, columns]], axis=0), bound, total)
        sums_c[:, a * SLOTS : (a + 1) * SLOTS] = (total - KNB * bound).astype(bf16)
    for a in range(2):
        tiles = inner_tiles(q, a, lambda i, j: inner[i, j])
        for part in range(KNB // WIDE):
            columns = slice(part * WIDE * SLOTS, (part + 1) * WIDE * SLOTS)
            gathered_d[a, :, columns] = pick(lane_rows(own_codes[a, q], part * WIDE, WIDE), tiles, []).astype(bf16)


def middle_early_kernel(wide, got_c, own_codes, geo_c, recv_w, full_w, sums_c, gathered_d, bounds_d):
    early_part(1, wide, got_c, own_codes, geo_c, recv_w, full_w, sums_c, gathered_d, bounds_d)


def last_early_kernel(own, got_a, got_b, got_c, own_codes, geo_c, recv_w, full_w, sums_c, gathered_d, bounds_d, inner):
    p, q = parities()
    for c in range(2):
        inner[1, c] = own[0, c]
        inner[2, c] = own[1, c]
        inner[3 * (1 - p), c] = got_a[c]
        inner[3 * p, c] = got_b[c]
    early_part(2, inner, got_c, own_codes, geo_c, recv_w, full_w, sums_c, gathered_d, bounds_d)


def late_part(t, own_all, got_d, own_codes, geo_d, sums_c, gathered_d, bounds_d, full_w, out_w, first_w, second_w):
    p, q = parities()
    sums = [sums_c[...]]
    for a in range(2):
        tiles = outer_tiles(q, a, lambda i: got_d[i])
        bound = bounds_d[:, a * SLOTS : (a + 1) * SLOTS]
        total = None
        for part in range(KNB // WIDE):
            columns = slice(part * WIDE * SLOTS, (part + 1) * WIDE * SLOTS)
            got = pick(lane_rows(own_codes[a, q], part * WIDE, WIDE), tiles[:-1], tiles[-1:]).astype(bf16)
            rows = jnp.concatenate([got + gathered_d[a, :, columns], geo_d[1 + a, :, columns]], axis=0)
            total = edge_sum(full_w[t], rows, bound, total)
        sums.append((total - KNB * bound).astype(bf16))
    return node_update(own_all, jnp.concatenate(sums, axis=1), out_w[t], first_w[t], second_w[t])


def middle_kernel(
    wide, got_d, own_codes, geo_d, sums_c, gathered_d, bounds_d, full_w, out_w, first_w, second_w,
    latent_out, send_a, send_b,
):
    p, q = parities()
    own_all = jnp.concatenate([wide[1 + a, s] for s in (1 - q, q) for a in range(2)], axis=1)
    latent = late_part(1, own_all, got_d, own_codes, geo_d, sums_c, gathered_d, bounds_d, full_w, out_w, first_w, second_w)
    for a in range(2):
        latent_out[a, 1 - q] = latent[:, a * SLOTS : (a + 1) * SLOTS]
        latent_out[a, q] = latent[:, (2 + a) * SLOTS : (3 + a) * SLOTS]
    for c in range(2):
        send_a[c] = latent_out[1 - p, c]
        send_b[c] = latent_out[p, c]


def last_kernel(
    own, got_d, own_codes, geo_d, sums_c, gathered_d, bounds_d, full_w, out_w, first_w, second_w,
    raw, position, velocity, dec_first, dec_second, out_velocity, out_position,
):
    p, q = parities()
    own_all = jnp.concatenate([own[a, s] for s in (1 - q, q) for a in range(2)], axis=1)
    latent = late_part(2, own_all, got_d, own_codes, geo_d, sums_c, gathered_d, bounds_d, full_w, out_w, first_w, second_w)
    hidden = jnp.maximum(tdot(dec_first[...], latent), 0.0).astype(bf16)
    accel = jnp.dot(dec_second[...], hidden, preferred_element_type=f32)
    for b in range(4):
        a, c = b % 2, (1 - q, q)[b // 2]
        live = raw[a, c, 32:PACK].astype(f32)[6:7]
        speed = velocity[a, c] + time_step * (accel[:, b * SLOTS : (b + 1) * SLOTS] * live)
        out_velocity[a, c] = speed
        out_position[a, c] = position[a, c] + time_step * speed


def run(kernel, name, out, scratch, operands, outside=(), work=None):
    vmem = pl.BlockSpec(memory_space=pltpu.VMEM)
    far = pl.BlockSpec(memory_space=pltpu.HBM)
    operands = [
        pltpu.with_memory_space_constraint(x, pltpu.HBM) if k in outside else x for k, x in enumerate(operands)
    ]
    return pl.pallas_call(
        kernel,
        out_shape=[jax.ShapeDtypeStruct(shape, dtype) for shape, dtype in out],
        in_specs=[far if k in outside else vmem for k in range(len(operands))],
        out_specs=[vmem] * len(out),
        scratch_shapes=[pltpu.VMEM(*entry) if isinstance(entry, tuple) else entry for entry in scratch],
        compiler_params=pltpu.CompilerParams(vmem_limit_bytes=32 << 20),
        cost_estimate=None if work is None else pl.CostEstimate(flops=work, bytes_accessed=4 << 20, transcendentals=0),
        name=name,
    )(*operands)


def swaps(count, start):
    pairs = []
    for low in range(start, count - 1, 2):
        pairs += [(low, low + 1), (low + 1, low)]
    return pairs


def swap(block, axis, start):
    return lax.ppermute(block, axis, swaps(lax.axis_size(axis), start))


def shards(
    features,
    position,
    velocity,
    occupancy,
    neighbor_codes,
    edge_mask,
    enc_first,
    enc_second,
    edge_recv,
    edge_send,
    edge_geo,
    edge_out,
    node_first,
    node_second,
    dec_first,
    dec_second,
):
    tile = (LAT, SLOTS)
    side = ((2, *tile), bf16)
    column = ((4, *tile), bf16)
    raw_column = ((6, PACK, SLOTS), bf16)
    steps = edge_recv.shape[0]
    whole = lambda values: (values.shape, values.dtype)
    geometry = ((4, GEO, KNB * SLOTS), bf16)
    early = [((EH, 2 * SLOTS), bf16), ((2, LAT, KNB * SLOTS), bf16), ((EH, 2 * SLOTS), f32)]

    features = jnp.transpose(features, (0, 2, 1, 3))
    inputs = (features, position, occupancy, neighbor_codes, edge_mask)
    raw, own_codes, send_a, send_b = run(
        prepare_kernel,
        "prepare",
        [((2, 2, PACK, SLOTS), bf16), ((2, 2, KNB, SLOTS), i32), side, side],
        [
            whole(position),
            pltpu.SMEM(occupancy.shape, i32),
            whole(neighbor_codes),
            whole(edge_mask),
            pltpu.SemaphoreType.DMA((4,)),
        ],
        inputs,
        range(1, 5),
    )
    got_a, got_b = swap(send_a, "slab", 0), swap(send_b, "slab", 1)
    plain = (
        edge_recv, edge_out, node_first, node_second, enc_second, dec_first, position, velocity
    )
    full_w, recv_w, out_w, first_w, second_w, enc_two, dec_one, place, speed = run(
        weights_kernel,
        "weights",
        [((steps, LAT + GEO, EH), bf16), *[whole(w) for w in plain]],
        [whole(edge_geo), pltpu.SemaphoreType.DMA((2 + len(plain),))],
        (own_codes, edge_send, edge_geo, *plain),
        range(1, 3 + len(plain)),
        1 << 30,
    )
    send_c, send_d = run(pack_raw_kernel, "pack_raw", [raw_column] * 2, [], (raw, got_a, got_b, enc_two))
    got_d, got_c = swap(send_d, "cross", 1), swap(send_c, "cross", 0)
    pack, codes_all, inner, bounds_d, sums_c, geo_c = run(
        first_early_kernel,
        "first_early",
        [
            ((6, 2, PACK, SLOTS), bf16),
            ((4, 2, KNB, SLOTS), i32),
            ((6, 2, *tile), bf16),
            ((EH, 4 * SLOTS), f32),
            ((EH, 4 * SLOTS), bf16),
            geometry,
        ],
        [((6, *tile), bf16), ((EH, 4 * SLOTS), f32)],
        (raw, got_a, got_b, got_c, own_codes, enc_first, enc_two, recv_w, full_w),
        (),
        1 << 31,
    )
    wide, geo_d, send_c, send_d = run(
        first_kernel,
        "first_step",
        [((4, 2, *tile), bf16), geometry, column, column],
        [((6, *tile), bf16), ((EH, 4 * SLOTS), bf16)],
        (pack, codes_all, inner, bounds_d, sums_c, got_d, enc_first, enc_two, full_w, out_w, first_w, second_w),
    )
    got_d, got_c = swap(send_d, "cross", 1), swap(send_c, "cross", 0)
    parts = run(
        middle_early_kernel, "middle_early", early, [], (wide, got_c, own_codes, geo_c, recv_w, full_w), (), 1 << 31
    )
    latent, send_a, send_b = run(
        middle_kernel,
        "middle_step",
        [((2, 2, *tile), bf16), side, side],
        [],
        (wide, got_d, own_codes, geo_d, *parts, full_w, out_w, first_w, second_w),
    )
    got_a, got_b = swap(send_a, "slab", 0), swap(send_b, "slab", 1)
    send_c, send_d = run(pack_kernel, "pack", [column] * 2, [], (latent, got_a, got_b))
    got_d, got_c = swap(send_d, "cross", 1), swap(send_c, "cross", 0)
    parts = run(
        last_early_kernel,
        "last_early",
        early,
        [((4, 2, *tile), bf16)],
        (latent, got_a, got_b, got_c, own_codes, geo_c, recv_w, full_w),
        (),
        1 << 31,
    )
    operands = (latent, got_d, own_codes, geo_d, *parts, full_w, out_w, first_w, second_w)
    return tuple(
        run(
            last_kernel,
            "last_step",
            [((2, 2, 2, SLOTS), f32)] * 2,
            [],
            (*operands, raw, place, speed, dec_one, dec_second.T),
        )
    )


def solution(mesh):
    tile = P("slab", "cross", None, None)
    return jax.shard_map(
        shards,
        mesh=mesh,
        in_specs=(tile, tile, tile, P("slab", "cross"), tile, tile) + (P(),) * 10,
        out_specs=(tile, tile),
        check_vma=False,
    )
```

```python
import functools

import jax
import jax.numpy as jnp
from jax import lax
from jax.experimental import pallas as pl
from jax.experimental.pallas import tpu as pltpu
from jax.sharding import PartitionSpec as P

time_step = 0.5
LAT = 128
EH = 512
INF = 30
KNB = 16
SLOTS = 128
PACK = 48
GEO = 32
WIDE = 8
UNROLL = 4
BLOCKED = -(2.0**40)
bf16 = jnp.bfloat16
f32 = jnp.float32
i32 = jnp.int32


def tdot(left, right):
    return lax.dot_general(left, right, (((0,), (0,)), ((), ())), preferred_element_type=f32)


def split3(values):
    high = values.astype(bf16).astype(f32)
    rest = values - high
    mid = rest.astype(bf16).astype(f32)
    return [high, mid, rest - mid]


def norm_rows(values):
    center = values - jnp.mean(values, axis=0, keepdims=True)
    spread = jnp.mean(center * center, axis=0, keepdims=True)
    return center * lax.rsqrt(spread + 1e-05)


def parities():
    return lax.rem(lax.axis_index("slab"), 2), lax.rem(lax.axis_index("cross"), 2)


def lane_rows(values, first, count):
    return jnp.concatenate([values[k : k + 1] for k in range(first, first + count)], axis=1)


def repeated(values, count):
    return jnp.concatenate([values] * count, axis=1)


def prepare_kernel(features_in, position_in, occupancy_in, codes_in, mask_in, raw, own_codes, send_a, send_b,
                   features, position, occupancy, codes, mask, sems):
    pairs = ((features_in, features), (position_in, position), (occupancy_in, occupancy), (codes_in, codes), (mask_in, mask))
    copies = [pltpu.make_async_copy(source, target, sems.at[k]) for k, (source, target) in enumerate(pairs)]
    for copy in copies:
        copy.start()
    p, q = parities()
    lane = lax.broadcasted_iota(i32, (1, SLOTS), 1)
    for copy in copies:
        copy.wait()
    for a in range(2):
        for c in range(2):
            live = (lane < occupancy[a, c]).astype(f32)
            rows = [features[a, :, c, :].astype(f32), jnp.zeros((2, SLOTS), f32)]
            rows += split3(position[a, c, 0:1]) + split3(position[a, c, 1:2])
            rows += [live, jnp.zeros((PACK - 39, SLOTS), f32)]
            raw[a, c] = jnp.concatenate(rows, axis=0).astype(bf16)
            own_codes[a, c] = jnp.where(mask[a, c] > 0, codes[a, c], (codes[a, c] & (SLOTS - 1)) - SLOTS)
    for near, far, out in ((1 - p, p, send_a), (p, 1 - p, send_b)):
        for c in range(2):
            out[c, 0:PACK] = raw[near, c]
            out[c, PACK : 2 * PACK] = raw[far, c]
            code = own_codes[near, c]
            out[c, 2 * PACK : 2 * PACK + KNB] = (code >> 7).astype(f32).astype(bf16)
            out[c, 2 * PACK + KNB :] = (code & (SLOTS - 1)).astype(f32).astype(bf16)


def weights_kernel(token, *refs):
    count = len(refs) // 2
    sources, outs, (geo_w, sems) = refs[:count], refs[count:-2], refs[-2:]
    full_w = outs[0]
    targets = (full_w.at[:, 0:LAT, :], geo_w, *outs[1:])
    copies = [pltpu.make_async_copy(source, target, sems.at[k]) for k, (source, target) in enumerate(zip(sources, targets))]
    for copy in copies:
        copy.start()
    for copy in copies:
        copy.wait()
    for t in range(full_w.shape[0]):
        values = geo_w[t]
        high = values.astype(bf16).astype(f32)
        low = values - high
        blank = jnp.zeros((5, EH), f32)
        rows = [high, jnp.full((1, EH), BLOCKED, f32), blank[:4], high, blank, low, blank, jnp.zeros((8, EH), f32)]
        full_w[t, LAT:, :] = jnp.concatenate(rows, axis=0).astype(bf16)


def pack_raw_kernel(own, got_a, got_b, token, send_c, send_d):
    p, q = parities()
    for j, out in ((1 - q, send_c), (q, send_d)):
        out[2] = own[0, j]
        out[3] = own[1, j]
        for side, got in ((1 - p, got_a), (p, got_b)):
            out[1 + 3 * side] = got[j, 0:PACK]
            out[5 * side] = got[j, PACK : 2 * PACK]


def pack_kernel(own, got_a, got_b, send_c, send_d):
    p, q = parities()
    for j, out in ((1 - q, send_c), (q, send_d)):
        out[1] = own[0, j]
        out[2] = own[1, j]
        out[3 * (1 - p)] = got_a[j]
        out[3 * p] = got_b[j]


def one_hot(window, slot, numbers):
    wide = slot.shape[1]
    iota = lax.broadcasted_iota(i32, (SLOTS, wide), 0).astype(jnp.int16)
    parts = []
    for number in numbers:
        wanted = jnp.where(window == number, slot, -1).astype(jnp.int16)
        hit = iota == jnp.broadcast_to(wanted, (SLOTS, wide))
        parts.append(jnp.where(hit, jnp.ones((), bf16), jnp.zeros((), bf16)))
    return jnp.concatenate(parts, axis=0)


def pick(codes, tiles, direct):
    window = codes >> 7
    slot = codes & (SLOTS - 1)
    hot = one_hot(window, slot, [number for number, _ in tiles])
    got = jnp.dot(jnp.concatenate([tile for _, tile in tiles], axis=1), hot, preferred_element_type=f32)
    parts = []
    for k in range(codes.shape[1] // SLOTS):
        lanes = slice(k * SLOTS, (k + 1) * SLOTS)
        part = got[:, lanes]
        index = jnp.broadcast_to(slot[:, lanes], part.shape)
        for number, tile in direct:
            here = jnp.broadcast_to(window[:, lanes], part.shape) == number
            moved = jnp.take_along_axis(tile.astype(f32), index, axis=1, mode="promise_in_bounds")
            part = jnp.where(here, moved, part)
        parts.append(part)
    return jnp.concatenate(parts, axis=1)


def inner_tiles(s, a, tile_of):
    return [(3 * d + 1 - s + j, tile_of(a + d, j)) for d in range(3) for j in range(2)]


def outer_tiles(s, a, tile_of):
    return [(3 * d + 2 * s, tile_of(a + d)) for d in range(3)]


def geometry_rows(got, own_x, own_y, own_live):
    delta_x = got[0:1] + got[1:2] + got[2:3] - own_x
    delta_y = got[3:4] + got[4:5] + got[5:6] - own_y
    distance = delta_x * delta_x + delta_y * delta_y
    blocked = 1.0 - own_live * got[6:7]
    values = jnp.concatenate([delta_x, delta_y, distance, blocked, jnp.zeros((4, got.shape[1]), f32)], axis=0)
    high = values.astype(bf16).astype(f32)
    return jnp.concatenate([high, values - high, high, jnp.zeros_like(high)], axis=0).astype(bf16)


def edge_sum(full_w, right_side, bound, total):
    hidden = tdot(full_w, right_side)
    for k in range(right_side.shape[1] // SLOTS):
        part = jnp.maximum(hidden[:, k * SLOTS : (k + 1) * SLOTS], bound)
        total = part if total is None else total + part
    return total


def node_update(own_all, sums, out_w, first_w, second_w):
    summed = tdot(out_w, sums).astype(bf16)
    joined = tdot(first_w, jnp.concatenate([own_all, summed], axis=0))
    joined = jnp.maximum(joined, 0.0).astype(bf16)
    update = norm_rows(tdot(second_w, joined))
    return (own_all.astype(f32) + update).astype(bf16)


def encoded(rows, enc_first, enc_second):
    weight = jnp.concatenate([enc_first[...], jnp.zeros((PACK - INF, LAT), bf16)], axis=0)
    raw = jnp.concatenate(rows, axis=1)
    hidden = jnp.maximum(tdot(weight, raw), 0.0).astype(bf16)
    return norm_rows(tdot(enc_second[...], hidden)).astype(bf16)


def first_bins(s, inner, pack_inner, outer, pack_outer, codes_all, bounds, full_w, sums, geo_out):
    def inner_tile(i, j):
        return jnp.concatenate([inner[i, j], pack_inner[i, j, 32:PACK, :]], axis=0)

    def outer_tile(i):
        return jnp.concatenate([outer[i], pack_outer[i, 32:PACK, :]], axis=0)

    def one_bin(a, carry):
        codes = codes_all[a, s]
        tiles = outer_tiles(s, a, outer_tile) + inner_tiles(s, a, inner_tile)
        me = pack_inner[a + 1, s, 32:PACK, :].astype(f32)
        own_x = repeated(me[0:1] + me[1:2] + me[2:3], WIDE)
        own_y = repeated(me[3:4] + me[4:5] + me[5:6], WIDE)
        own_live = repeated(me[6:7], WIDE)
        columns = pl.ds(pl.multiple_of(a * SLOTS, SLOTS), SLOTS)
        bound = bounds[:, columns]
        total = None
        for part in range(KNB // WIDE):
            got = pick(lane_rows(codes, part * WIDE, WIDE), tiles[:-1], tiles[-1:])
            geo = geometry_rows(got[LAT:], own_x, own_y, own_live)
            geo_out[a, :, part * WIDE * SLOTS : (part + 1) * WIDE * SLOTS] = geo
            total = edge_sum(full_w[0], jnp.concatenate([got[:LAT].astype(bf16), geo], axis=0), bound, total)
        sums[:, columns] = (total - KNB * bound).astype(bf16)
        return carry

    lax.fori_loop(0, 4, one_bin, 0, unroll=UNROLL)


def first_early_kernel(
    own, got_a, got_b, got_c, own_codes, enc_first, enc_second, recv_w, full_w,
    pack, codes_all, inner, bounds_d, sums_c, geo_c, outer, bounds_c,
):
    p, q = parities()
    for c in range(2):
        for a in range(2):
            pack[2 + a, c] = own[a, c]
            codes_all[1 + a, c] = own_codes[a, c]
        for side, got in ((1 - p, got_a), (p, got_b)):
            pack[1 + 3 * side, c] = got[c, 0:PACK]
            pack[5 * side, c] = got[c, PACK : 2 * PACK]
            window = got[c, 2 * PACK : 2 * PACK + KNB].astype(f32)
            slot = got[c, 2 * PACK + KNB :].astype(f32)
            codes_all[3 * side, c] = (window * SLOTS + slot).astype(i32)
    for i in range(0, 6, 2):
        rows = [pack[i + j // 2, j % 2] for j in range(4)] + [got_c[i], got_c[i + 1]]
        latent = encoded(rows, enc_first, enc_second)
        for j in range(4):
            inner[i + j // 2, j % 2] = latent[:, j * SLOTS : (j + 1) * SLOTS]
        for j in range(2):
            outer[i + j] = latent[:, (4 + j) * SLOTS : (5 + j) * SLOTS]
    for s, bounds in ((1 - q, bounds_c), (q, bounds_d)):
        bounds[...] = -tdot(recv_w[0], jnp.concatenate([inner[1 + a, s] for a in range(4)], axis=1))
    first_bins(1 - q, inner, pack, outer, got_c, codes_all, bounds_c, full_w, sums_c, geo_c)


def first_kernel(
    pack, codes_all, inner, bounds_d, sums_c, got_d, enc_first, enc_second, full_w, out_w, first_w, second_w,
    latent_out, geo_d, send_c, send_d, outer, sums_d,
):
    p, q = parities()
    latent = encoded([got_d[i] for i in range(6)], enc_first, enc_second)
    for i in range(6):
        outer[i] = latent[:, i * SLOTS : (i + 1) * SLOTS]
    first_bins(q, inner, pack, outer, got_d, codes_all, bounds_d, full_w, sums_d, geo_d)
    own_all = jnp.concatenate([inner[1 + a, s] for s in (1 - q, q) for a in range(4)], axis=1)
    sums = jnp.concatenate([sums_c[...], sums_d[...]], axis=1)
    latent = node_update(own_all, sums, out_w[0], first_w[0], second_w[0])
    for i in range(4):
        for s, send, at in ((1 - q, send_c, i), (q, send_d, 4 + i)):
            tile = latent[:, at * SLOTS : (at + 1) * SLOTS]
            send[i] = tile
            latent_out[i, s] = tile


def early_part(t, inner, got_c, own_codes, geo_c, recv_w, full_w, sums_c, gathered_d, bounds_d):
    p, q = parities()
    outs = [-tdot(recv_w[t], jnp.concatenate([inner[1, s], inner[2, s]], axis=1)) for s in (1 - q, q)]
    bounds_d[...] = outs[1]
    for a in range(2):
        bound = outs[0][:, a * SLOTS : (a + 1) * SLOTS]
        tiles = outer_tiles(1 - q, a, lambda i: got_c[i]) + inner_tiles(1 - q, a, lambda i, j: inner[i, j])
        total = None
        for part in range(KNB // WIDE):
            columns = slice(part * WIDE * SLOTS, (part + 1) * WIDE * SLOTS)
            got = pick(lane_rows(own_codes[a, 1 - q], part * WIDE, WIDE), tiles[:-1], tiles[-1:]).astype(bf16)
            total = edge_sum(full_w[t], jnp.concatenate([got, geo_c[1 + a, :, columns]], axis=0), bound, total)
        sums_c[:, a * SLOTS : (a + 1) * SLOTS] = (total - KNB * bound).astype(bf16)
    for a in range(2):
        tiles = inner_tiles(q, a, lambda i, j: inner[i, j])
        for part in range(KNB // WIDE):
            columns = slice(part * WIDE * SLOTS, (part + 1) * WIDE * SLOTS)
            gathered_d[a, :, columns] = pick(lane_rows(own_codes[a, q], part * WIDE, WIDE), tiles, []).astype(bf16)


def middle_early_kernel(wide, got_c, own_codes, geo_c, recv_w, full_w, sums_c, gathered_d, bounds_d):
    early_part(1, wide, got_c, own_codes, geo_c, recv_w, full_w, sums_c, gathered_d, bounds_d)


def last_early_kernel(own, got_a, got_b, got_c, own_codes, geo_c, recv_w, full_w, sums_c, gathered_d, bounds_d, inner):
    p, q = parities()
    for c in range(2):
        inner[1, c] = own[0, c]
        inner[2, c] = own[1, c]
        inner[3 * (1 - p), c] = got_a[c]
        inner[3 * p, c] = got_b[c]
    early_part(2, inner, got_c, own_codes, geo_c, recv_w, full_w, sums_c, gathered_d, bounds_d)


def late_part(t, own_all, got_d, own_codes, geo_d, sums_c, gathered_d, bounds_d, full_w, out_w, first_w, second_w):
    p, q = parities()
    sums = [sums_c[...]]
    for a in range(2):
        tiles = outer_tiles(q, a, lambda i: got_d[i])
        bound = bounds_d[:, a * SLOTS : (a + 1) * SLOTS]
        total = None
        for part in range(KNB // WIDE):
            columns = slice(part * WIDE * SLOTS, (part + 1) * WIDE * SLOTS)
            got = pick(lane_rows(own_codes[a, q], part * WIDE, WIDE), tiles[:-1], tiles[-1:]).astype(bf16)
            rows = jnp.concatenate([got + gathered_d[a, :, columns], geo_d[1 + a, :, columns]], axis=0)
            total = edge_sum(full_w[t], rows, bound, total)
        sums.append((total - KNB * bound).astype(bf16))
    return node_update(own_all, jnp.concatenate(sums, axis=1), out_w[t], first_w[t], second_w[t])


def middle_kernel(
    wide, got_d, own_codes, geo_d, sums_c, gathered_d, bounds_d, full_w, out_w, first_w, second_w,
    latent_out, send_a, send_b,
):
    p, q = parities()
    own_all = jnp.concatenate([wide[1 + a, s] for s in (1 - q, q) for a in range(2)], axis=1)
    latent = late_part(1, own_all, got_d, own_codes, geo_d, sums_c, gathered_d, bounds_d, full_w, out_w, first_w, second_w)
    for a in range(2):
        latent_out[a, 1 - q] = latent[:, a * SLOTS : (a + 1) * SLOTS]
        latent_out[a, q] = latent[:, (2 + a) * SLOTS : (3 + a) * SLOTS]
    for c in range(2):
        send_a[c] = latent_out[1 - p, c]
        send_b[c] = latent_out[p, c]


def last_kernel(
    own, got_d, own_codes, geo_d, sums_c, gathered_d, bounds_d, full_w, out_w, first_w, second_w,
    raw, position, velocity, dec_first, dec_second, out_velocity, out_position,
):
    p, q = parities()
    own_all = jnp.concatenate([own[a, s] for s in (1 - q, q) for a in range(2)], axis=1)
    latent = late_part(2, own_all, got_d, own_codes, geo_d, sums_c, gathered_d, bounds_d, full_w, out_w, first_w, second_w)
    hidden = jnp.maximum(tdot(dec_first[...], latent), 0.0).astype(bf16)
    accel = jnp.dot(dec_second[...], hidden, preferred_element_type=f32)
    for b in range(4):
        a, c = b % 2, (1 - q, q)[b // 2]
        live = raw[a, c, 32:PACK].astype(f32)[6:7]
        speed = velocity[a, c] + time_step * (accel[:, b * SLOTS : (b + 1) * SLOTS] * live)
        out_velocity[a, c] = speed
        out_position[a, c] = position[a, c] + time_step * speed


def run(kernel, name, out, scratch, operands, outside=(), work=None):
    vmem = pl.BlockSpec(memory_space=pltpu.VMEM)
    far = pl.BlockSpec(memory_space=pltpu.HBM)
    operands = [
        pltpu.with_memory_space_constraint(x, pltpu.HBM) if k in outside else x for k, x in enumerate(operands)
    ]
    return pl.pallas_call(
        kernel,
        out_shape=[jax.ShapeDtypeStruct(shape, dtype) for shape, dtype in out],
        in_specs=[far if k in outside else vmem for k in range(len(operands))],
        out_specs=[vmem] * len(out),
        scratch_shapes=[pltpu.VMEM(*entry) if isinstance(entry, tuple) else entry for entry in scratch],
        compiler_params=pltpu.CompilerParams(vmem_limit_bytes=32 << 20),
        cost_estimate=None if work is None else pl.CostEstimate(flops=work, bytes_accessed=4 << 20, transcendentals=0),
        name=name,
    )(*operands)


def swaps(count, start):
    pairs = []
    for low in range(start, count - 1, 2):
        pairs += [(low, low + 1), (low + 1, low)]
    return pairs


def swap(block, axis, start):
    return lax.ppermute(block, axis, swaps(lax.axis_size(axis), start))


def shards(
    features,
    position,
    velocity,
    occupancy,
    neighbor_codes,
    edge_mask,
    enc_first,
    enc_second,
    edge_recv,
    edge_send,
    edge_geo,
    edge_out,
    node_first,
    node_second,
    dec_first,
    dec_second,
):
    tile = (LAT, SLOTS)
    side = ((2, *tile), bf16)
    column = ((4, *tile), bf16)
    raw_column = ((6, PACK, SLOTS), bf16)
    steps = edge_recv.shape[0]
    whole = lambda values: (values.shape, values.dtype)
    geometry = ((4, GEO, KNB * SLOTS), bf16)
    early = [((EH, 2 * SLOTS), bf16), ((2, LAT, KNB * SLOTS), bf16), ((EH, 2 * SLOTS), f32)]

    features = jnp.transpose(features, (0, 2, 1, 3))
    inputs = (features, position, occupancy, neighbor_codes, edge_mask)
    raw, own_codes, send_a, send_b = run(
        prepare_kernel,
        "prepare",
        [((2, 2, PACK, SLOTS), bf16), ((2, 2, KNB, SLOTS), i32), side, side],
        [
            whole(features),
            whole(position),
            pltpu.SMEM(occupancy.shape, i32),
            whole(neighbor_codes),
            whole(edge_mask),
            pltpu.SemaphoreType.DMA((5,)),
        ],
        inputs,
        range(5),
    )
    got_a, got_b = swap(send_a, "slab", 0), swap(send_b, "slab", 1)
    plain = (
        edge_recv, edge_out, node_first, node_second, enc_first, enc_second, dec_first, dec_second.T, position, velocity
    )
    full_w, recv_w, out_w, first_w, second_w, enc_one, enc_two, dec_one, dec_two, place, speed = run(
        weights_kernel,
        "weights",
        [((steps, LAT + GEO, EH), bf16), *[whole(w) for w in plain]],
        [whole(edge_geo), pltpu.SemaphoreType.DMA((2 + len(plain),))],
        (own_codes, edge_send, edge_geo, *plain),
        range(1, 3 + len(plain)),
        1 << 30,
    )
    send_c, send_d = run(pack_raw_kernel, "pack_raw", [raw_column] * 2, [], (raw, got_a, got_b, enc_one))
    got_d, got_c = swap(send_d, "cross", 1), swap(send_c, "cross", 0)
    pack, codes_all, inner, bounds_d, sums_c, geo_c = run(
        first_early_kernel,
        "first_early",
        [
            ((6, 2, PACK, SLOTS), bf16),
            ((4, 2, KNB, SLOTS), i32),
            ((6, 2, *tile), bf16),
            ((EH, 4 * SLOTS), f32),
            ((EH, 4 * SLOTS), bf16),
            geometry,
        ],
        [((6, *tile), bf16), ((EH, 4 * SLOTS), f32)],
        (raw, got_a, got_b, got_c, own_codes, enc_one, enc_two, recv_w, full_w),
        (),
        1 << 31,
    )
    wide, geo_d, send_c, send_d = run(
        first_kernel,
        "first_step",
        [((4, 2, *tile), bf16), geometry, column, column],
        [((6, *tile), bf16), ((EH, 4 * SLOTS), bf16)],
        (pack, codes_all, inner, bounds_d, sums_c, got_d, enc_one, enc_two, full_w, out_w, first_w, second_w),
    )
    got_d, got_c = swap(send_d, "cross", 1), swap(send_c, "cross", 0)
    parts = run(
        middle_early_kernel, "middle_early", early, [], (wide, got_c, own_codes, geo_c, recv_w, full_w), (), 1 << 31
    )
    latent, send_a, send_b = run(
        middle_kernel,
        "middle_step",
        [((2, 2, *tile), bf16), side, side],
        [],
        (wide, got_d, own_codes, geo_d, *parts, full_w, out_w, first_w, second_w),
    )
    got_a, got_b = swap(send_a, "slab", 0), swap(send_b, "slab", 1)
    send_c, send_d = run(pack_kernel, "pack", [column] * 2, [], (latent, got_a, got_b))
    got_d, got_c = swap(send_d, "cross", 1), swap(send_c, "cross", 0)
    parts = run(
        last_early_kernel,
        "last_early",
        early,
        [((4, 2, *tile), bf16)],
        (latent, got_a, got_b, got_c, own_codes, geo_c, recv_w, full_w),
        (),
        1 << 31,
    )
    operands = (latent, got_d, own_codes, geo_d, *parts, full_w, out_w, first_w, second_w)
    return tuple(
        run(
            last_kernel,
            "last_step",
            [((2, 2, 2, SLOTS), f32)] * 2,
            [],
            (*operands, raw, place, speed, dec_one, dec_two),
        )
    )


def solution(mesh):
    tile = P("slab", "cross", None, None)
    return jax.shard_map(
        shards,
        mesh=mesh,
        in_specs=(tile, tile, tile, P("slab", "cross"), tile, tile) + (P(),) * 10,
        out_specs=(tile, tile),
        check_vma=False,
    )
```
